512 devices in a mesh: ctx: 32 (over z_lo, x), head: 4 (over z_hi, core), qry: 4 (over y).
Axes of the slice: x: 4, y: 4, z: 16 (z_hi: 2, z_lo: 8; z = z_hi * 8 + z_lo), core: 2. Of those that a mesh axis runs over, the one named last changes fastest.
Arguments:
- queries: bfloat16 [4096, 4, 896], P(('qry', 'ctx'), 'head'), may hold values from -110 to 110
- key_cache: bfloat16 [4, 8192, 128], P('head', 'ctx'), may hold values from -4 to 4
- key_positions: int32 [8192], P('ctx'), may hold values from 0 to 8191, each once
- span_end: int32 [4096], P(('qry', 'ctx')), may hold values from 2048 to 8192, as said below
Outputs:
- importance: float32 [4, 8192], P('head', 'ctx')
The draws below stay inside these ranges and needn't reach their ends.
Inputs may be any that keep to these rules, and one draw needn't show every extreme that they name: `span_end`: constant over each of 16 runs of 256 consecutive queries, nondecreasing; the first run ends at 2048, the last at 8192.
All inputs are finite; a program needn't handle non-finite values.
Results may differ from the reference program's by a relative error of at most 0.0003.
Values may be sent and summed in bfloat16 or wider, within the bound.
A program may use at most 64 MiB of HBM per device.

```python
import math
import jax
import jax.numpy as jnp
from jax import lax

KV_HEADS = 4
GROUP = 7
HEAD_DIM = 128
KEYS = 8192
QUERIES = 4096


def mixed_values(key, shape):
    normal_part = jax.random.normal(key, shape, jnp.float32)
    return normal_part


def key_mixture(key):
    centres = mixed_values(jax.random.fold_in(key, 21), (KV_HEADS, 64, HEAD_DIM))
    noise = mixed_values(jax.random.fold_in(key, 22), (KV_HEADS, KEYS, HEAD_DIM))
    first = jax.random.randint(jax.random.fold_in(key, 23), (KV_HEADS, KEYS), 0, 64)
    second = jax.random.randint(jax.random.fold_in(key, 24), (KV_HEADS, KEYS), 0, 64)
    owner = jnp.minimum(first, second)
    log_scales = jax.random.uniform(jax.random.fold_in(key, 25), (KV_HEADS, 64), jnp.float32, math.log(0.7), math.log(1.4))
    scales = jnp.exp(log_scales)
    head_index = jnp.arange(KV_HEADS)[:, None]
    picked = centres[head_index, owner]
    key_scale = scales[head_index, owner]
    cache_rows = jnp.clip(key_scale[:, :, None] * (picked + 0.5 * noise), -4.0, 4.0)
    return cache_rows


def draw_key_cache(key, part):
    cache_rows = key_mixture(key)
    return cache_rows.astype(jnp.bfloat16)


def draw_queries(key, part):
    key = jax.random.fold_in(key, 7)
    values = jnp.clip(jax.random.normal(key, (QUERIES, KV_HEADS, GROUP * HEAD_DIM), jnp.float32), -5.0, 5.0)
    return values.astype(jnp.bfloat16)


def draw_span_end(key, part):
    key = jax.random.fold_in(key, 11)
    bounds = jnp.sort(jax.random.randint(key, (16,), KEYS // 4, KEYS + 1))
    bounds = bounds.at[0].set(KEYS // 4).at[15].set(KEYS)
    owner = jnp.arange(QUERIES) * 16 // QUERIES
    return bounds[owner].astype(jnp.int32)


def setup_inputs(seed: int = 0) -> dict:
    keys = jax.random.split(jax.random.key(seed), 5)
    return {
        "queries": draw_queries(jax.random.fold_in(keys[4], 71), 0),
        "key_cache": draw_key_cache(jax.random.fold_in(keys[4], 71), 0),
        "key_positions": jax.random.permutation(keys[2], KEYS).astype(jnp.int32),
        "span_end": draw_span_end(jax.random.fold_in(keys[4], 71), 0),
    }


NEG_FILL = -1e30


def reference(queries, key_cache, key_positions, span_end):
    block_rows = min(512, QUERIES)
    blocks = QUERIES // block_rows
    score_scale = HEAD_DIM ** -0.5

    def per_head(head_index):
        cache_rows = key_cache[head_index].astype(jnp.float32)
        head_rows = queries[:, head_index, :].reshape(blocks, block_rows, GROUP * HEAD_DIM)
        head_ends = span_end.reshape(blocks, block_rows)

        def one_block(running, inputs):
            query_block, end_block = inputs
            visible = key_positions[None, :] < end_block[:, None]
            for member in range(GROUP):
                part = query_block[:, member * HEAD_DIM:(member + 1) * HEAD_DIM].astype(jnp.float32)
                scores = jnp.dot(part, cache_rows.T, preferred_element_type=jnp.float32) * score_scale
                masked = jnp.where(visible, scores, NEG_FILL)
                peaks = jnp.max(masked, axis=1, keepdims=True)
                masses = jnp.sum(jnp.where(visible, jnp.exp(masked - peaks), 0.0), axis=1, keepdims=True)
                log_totals = peaks + jnp.log(masses)
                running = jnp.maximum(running, jnp.max(jnp.where(visible, scores - log_totals, NEG_FILL), axis=0))
            return running, None

        initial = jnp.full((KEYS,), NEG_FILL, jnp.float32)
        result, unused = lax.scan(one_block, initial, (head_rows, head_ends))
        return result

    return lax.map(per_head, jnp.arange(KV_HEADS))
```

```python
import functools
import math

import jax
import jax.numpy as jnp
from jax import lax
from jax.experimental import pallas as pl
from jax.experimental.pallas import tpu as pltpu
from jax.sharding import PartitionSpec as P

NEG_FILL = -1e30
MESH = pl.DeviceIdType.MESH
NX, NY, NZ = 4, 4, 8
PAIRS = NZ // 2


def kernel(group, q_ref, k_ref, p_ref, e_ref, o_ref, qbuf, kbuf, pbuf, ebuf, sbuf, mst, lst, colb, st, cm, rbuf,
           loc, qs, qr, kr, pr, ks, ps, yr, ys, ss, sr, cs, cr):
    ctx, y = lax.axis_index("ctx"), lax.axis_index("qry")
    z, x = ctx // NX, lax.rem(ctx, NX)
    keys, width = k_ref.shape
    quarter = keys // NY
    rows = qbuf.shape[0] * qbuf.shape[1]
    scale = width**-0.5
    to_exp2 = math.log2(math.e) * scale
    mine = pl.ds(pl.multiple_of(y * quarter, quarter), quarter)

    def xdev(d):
        return {"ctx": z * NX + lax.rem(x + d, NX)}

    def ydev(d):
        return {"qry": lax.rem(y + d, NY)}

    def zdev(target):
        return {"ctx": target * NX + x}

    def remote(src, dst, send, recv, dev):
        return pltpu.make_async_remote_copy(src_ref=src, dst_ref=dst, send_sem=send, recv_sem=recv, device_id=dev, device_id_type=MESH)

    def drain(ref, sem):
        pltpu.make_async_copy(ref, ref, sem).wait()

    barrier = pltpu.get_barrier_semaphore()

    def greet(dev):
        pl.semaphore_signal(barrier, inc=1, device_id=dev, device_id_type=MESH)

    @pl.when(z > 0)
    def _():
        greet(zdev(z - 1))

    @pl.when(z < NZ - 1)
    def _():
        greet(zdev(z + 1))

    for d in (1, 3, 2):
        greet(xdev(d))
        greet(ydev(d))

    local = [
        pltpu.make_async_copy(k_ref.at[mine], kbuf.at[z, mine], loc.at[0]),
        pltpu.make_async_copy(p_ref, pbuf.at[z], loc.at[1]),
        pltpu.make_async_copy(q_ref, qbuf.at[x], loc.at[2]),
        pltpu.make_async_copy(e_ref, ebuf, loc.at[3]),
    ]
    for c in local:
        c.start()
    mst[...] = jnp.full(mst.shape, NEG_FILL, jnp.float32)
    lst[...] = jnp.zeros(lst.shape, jnp.float32)
    st[x] = jnp.zeros(st.shape[1:], jnp.float32)
    ends = jnp.where((z > 0) & (z < NZ - 1), 2, 1)
    pl.semaphore_wait(barrier, ends + 6)

    def send_block(src_k, src_p, block, target):
        remote(src_k, kbuf.at[block, mine], ks.at[0], kr.at[block], zdev(target)).start()
        remote(src_p, pbuf.at[block], ps.at[0], pr.at[block], zdev(target)).start()

    def wait_block(block):
        drain(kbuf.at[block, mine], kr.at[block])
        drain(pbuf.at[block], pr.at[block])

    def fan_out(g):
        part = kbuf.at[pl.ds(2 * g, 2), mine]
        for d in (1, 3, 2):
            remote(part, part, ys.at[0], yr.at[g], ydev(d)).start()

    for i in range(NZ):

        @pl.when((z == i) & (z < NZ - 1))
        def _():
            send_block(k_ref.at[mine], p_ref, z, z + 1)

        @pl.when(z > i)
        def _():
            wait_block(i)

            @pl.when(z < NZ - 1)
            def _():
                send_block(kbuf.at[i, mine], pbuf.at[i], i, z + 1)

        if i == 0:
            for j in range(NZ - 1):

                @pl.when(z > j)
                def _():
                    send_block(k_ref.at[mine], p_ref, z, j)

            for d in (1, 3, 2):
                remote(q_ref, qbuf.at[x], qs.at[0], qr.at[0], xdev(d)).start()
            local[0].wait()
            local[1].wait()

        if i % 2:

            @pl.when(z >= i)
            def _():
                fan_out(i // 2)

    def late(g):
        @pl.when(z < 2 * g)
        def _():
            wait_block(2 * g)

        @pl.when(z < 2 * g + 1)
        def _():
            wait_block(2 * g + 1)
            fan_out(g)

    late(0)
    local[2].wait()
    local[3].wait()
    drain(qbuf.at[pl.ds(0, NX - 1)], qr.at[0])
    end = ebuf[0:1, 0:1]

    def bias_of(g):
        pos = jnp.concatenate([pbuf[2 * g], pbuf[2 * g + 1]], axis=1)
        return jnp.where(pos < end, 0.0, NEG_FILL)

    def scan_pair(g, unused):
        @pl.when(g < PAIRS - 1)
        def _():
            late(g + 1)

        drain(kbuf.at[pl.ds(0, 2), pl.ds(0, (NY - 1) * quarter)], yr.at[g])
        part = kbuf[pl.ds(2 * g, 2)].reshape(2 * keys, width)
        bias = bias_of(g)
        for m in range(group):
            qm = qbuf[:, :, m * width : (m + 1) * width].reshape(rows, width)
            s = lax.dot_general(qm, part, (((1,), (1,)), ((), ())), preferred_element_type=jnp.float32)
            sbuf[g, m] = s
            t = s + bias
            pieces = [t[:, c * 128 : (c + 1) * 128] for c in range(2 * keys // 128)]
            old = mst[m]
            new = functools.reduce(jnp.maximum, pieces, old)
            total = lst[m] * jnp.exp2((old - new) * to_exp2)
            for piece in pieces:
                total = total + jnp.exp2((piece - new) * to_exp2)
            mst[m] = new
            lst[m] = total
        return unused

    lax.fori_loop(0, PAIRS, scan_pair, 0)

    eye = lax.broadcasted_iota(jnp.int32, (rows, 128), 0) == lax.broadcasted_iota(jnp.int32, (rows, 128), 1)
    for m in range(group):
        tops = mst[m]
        top = jnp.max(tops, axis=1, keepdims=True)
        mass = jnp.sum(lst[m] * jnp.exp2((tops - top) * to_exp2), axis=1, keepdims=True)
        st[x, m : m + 1] = jnp.sum(jnp.where(eye, top, 0.0), axis=0, keepdims=True)
        st[x, 8 + m : 9 + m] = jnp.sum(jnp.where(eye, mass, 0.0), axis=0, keepdims=True)
    for d in (1, 3, 2):
        remote(st.at[x], st.at[x], ss.at[0], sr.at[0], xdev(d)).start()
    drain(st.at[pl.ds(0, NX - 1)], sr.at[0])
    tops, masses = st[:, 0:8], st[:, 8:16]
    top = jnp.max(tops, axis=0)
    mass = jnp.sum(masses * jnp.exp2((tops - top[None]) * to_exp2), axis=0)
    total = top + jnp.log(mass) * (1.0 / scale)
    for m in range(group):
        col = jnp.sum(jnp.where(eye, total[m : m + 1], 0.0), axis=1, keepdims=True)
        colb[m] = jnp.broadcast_to(col, (rows, 128))

    def best_pair(g, unused):
        def member(m, acc):
            for r in range(rows // 8):
                col = colb[m, r * 8 : (r + 1) * 8]
                acc = tuple(
                    jnp.maximum(a, sbuf[g, m, r * 8 : (r + 1) * 8, c * 128 : (c + 1) * 128] - col)
                    for c, a in enumerate(acc)
                )
            return acc

        start = tuple(jnp.full((8, 128), NEG_FILL, jnp.float32) for c in range(2 * keys // 128))
        acc = lax.fori_loop(0, group, member, start)
        best = jnp.concatenate([jnp.max(a, axis=0, keepdims=True) for a in acc], axis=1) * scale
        best = jnp.where(bias_of(g) < 0.0, NEG_FILL, best)
        cm[2 * g] = best[:, :keys]
        cm[2 * g + 1] = best[:, keys:]
        return unused

    lax.fori_loop(0, PAIRS, best_pair, 0)

    def owner(step, unused):
        far_z = lax.rem(z + step // NY, NZ)
        far_y = lax.rem(y + lax.rem(step, NY), NY)
        remote(cm.at[far_z], rbuf.at[z * NY + y], cs.at[0], cr.at[0], {"ctx": far_z * NX + x, "qry": far_y}).start()
        return unused

    lax.fori_loop(1, NZ * NY, owner, 0)
    rbuf[z * NY + y] = cm[z]
    drain(rbuf.at[pl.ds(0, NZ * NY - 1)], cr.at[0])
    o_ref[...] = jnp.max(rbuf[...], axis=0)

    drain(rbuf.at[pl.ds(0, NZ * NY - 1)], cs.at[0])
    drain(st.at[pl.ds(0, NX - 1)], ss.at[0])
    drain(qbuf.at[pl.ds(0, NX - 1)], qs.at[0])
    drain(kbuf.at[pl.ds(0, 6)], ys.at[0])
    for v in range(NZ):
        count = 2 * v + 1 if v < NZ - 1 else v

        @pl.when(z == v)
        def _():
            drain(sbuf.at[0, 0, pl.ds(0, count * 8)], ks.at[0])
            drain(rbuf.at[pl.ds(0, count)], ps.at[0])


def shards(queries, key_cache, key_positions, span_end):
    own, unused, lanes = queries.shape
    keys, width = key_cache.shape[1:]
    group = lanes // width
    rows = own * NX
    dma = lambda n: pltpu.SemaphoreType.DMA((n,))
    return pl.pallas_call(
        functools.partial(kernel, group),
        out_shape=jax.ShapeDtypeStruct((1, keys), jnp.float32),
        in_specs=[pl.BlockSpec(memory_space=pl.ANY)] * 4,
        out_specs=pl.BlockSpec(memory_space=pltpu.VMEM),
        scratch_shapes=[
            pltpu.VMEM((NX, own, lanes), jnp.bfloat16),
            pltpu.VMEM((NZ, keys, width), jnp.bfloat16),
            pltpu.VMEM((NZ, 1, keys), jnp.int32),
            pltpu.VMEM((1, own), jnp.int32),
            pltpu.VMEM((PAIRS, group, rows, 2 * keys), jnp.float32),
            pltpu.VMEM((group, rows, 128), jnp.float32),
            pltpu.VMEM((group, rows, 128), jnp.float32),
            pltpu.VMEM((group, rows, 128), jnp.float32),
            pltpu.VMEM((NX, 16, 128), jnp.float32),
            pltpu.VMEM((NZ, 1, keys), jnp.float32),
            pltpu.VMEM((NZ * NY, 1, keys), jnp.float32),
            dma(4), dma(1), dma(1), dma(NZ), dma(NZ), dma(1), dma(1), dma(PAIRS), dma(1), dma(1), dma(1), dma(1), dma(1),
        ],
        compiler_params=pltpu.CompilerParams(collective_id=0, has_side_effects=True, vmem_limit_bytes=58 << 20),
    )(queries[:, 0], key_cache[0], key_positions[None], span_end[None])


def solution(mesh):
    placed = (P(("qry", "ctx"), "head", None), P("head", "ctx", None), P("ctx"), P(("qry", "ctx")))
    return jax.shard_map(shards, mesh=mesh, in_specs=placed, out_specs=P("head", "ctx"), check_vma=False)
```

```python
import functools
import math

import jax
import jax.numpy as jnp
from jax import lax
from jax.experimental import pallas as pl
from jax.experimental.pallas import tpu as pltpu
from jax.sharding import PartitionSpec as P

NEG_FILL = -1e30
MESH = pl.DeviceIdType.MESH
NX, NY, NZ = 4, 4, 8
HALF = NZ // 2


def kernel(group, q_ref, k_ref, p_ref, e_ref, o_ref, qbuf, kbuf, pbuf, ebuf, sbuf, mst, lst, colb, st, cm, rbuf,
           lq, le, qr, qz, qs, kr, pr, ks, ps, yr, ys, ss, sr, cs, cr):
    ctx, y = lax.axis_index("ctx"), lax.axis_index("qry")
    z, x = ctx // NX, lax.rem(ctx, NX)
    side = lax.rem(z, 2)
    twin = z + 1 - 2 * side
    half = z // HALF
    inside = side == half
    keys, width = k_ref.shape
    quarter = keys // NY
    rows = 2 * qbuf.shape[1] * qbuf.shape[2]
    scale = width**-0.5
    to_exp2 = math.log2(math.e) * scale
    mine = pl.ds(pl.multiple_of(y * quarter, quarter), quarter)

    def at(zz, xx):
        return {"ctx": zz * NX + xx}

    def turn(v, d):
        return lax.rem(v + d, 4)

    def remote(src, dst, send, recv, dev):
        return pltpu.make_async_remote_copy(src_ref=src, dst_ref=dst, send_sem=send, recv_sem=recv, device_id=dev, device_id_type=MESH)

    def drain(ref, sem):
        pltpu.make_async_copy(ref, ref, sem).wait()

    barrier = pltpu.get_barrier_semaphore()

    def greet(dev):
        pl.semaphore_signal(barrier, inc=1, device_id=dev, device_id_type=MESH)

    for j in range(HALF):
        source = HALF * side + j

        @pl.when(source != z)
        def _():
            greet(at(source, x))

    for d in (1, 3, 2):
        greet({"qry": turn(y, d)})
        greet(at(z, turn(x, d)))
    greet(at(twin, x))

    pltpu.make_async_copy(q_ref, qbuf.at[side, x], lq.at[0]).start()
    pltpu.make_async_copy(e_ref, ebuf, le.at[0]).start()
    slot = lax.rem(z, HALF)

    @pl.when(inside)
    def _():
        pltpu.make_async_copy(k_ref.at[mine], kbuf.at[y, slot], kr.at[slot // 2]).start()
        pltpu.make_async_copy(p_ref, pbuf.at[slot], pr.at[0]).start()

    mst[...] = jnp.full(mst.shape, NEG_FILL, jnp.float32)
    lst[...] = jnp.zeros(lst.shape, jnp.float32)
    st[side, x] = jnp.zeros(st.shape[2:], jnp.float32)
    pl.semaphore_wait(barrier, jnp.where(inside, 10, 11))

    remote(q_ref, qbuf.at[side, x], qs.at[0], qz.at[0], at(twin, x)).start()
    for i in range(HALF):
        target = 2 * i + half

        @pl.when(target != z)
        def _():
            remote(k_ref.at[mine], kbuf.at[y, slot], ks.at[0], kr.at[slot // 2], at(target, x)).start()
            remote(p_ref, pbuf.at[slot], ps.at[0], pr.at[0], at(target, x)).start()

    for d in (1, 3, 2):
        remote(q_ref, qbuf.at[side, x], qs.at[0], qr.at[0], at(z, turn(x, d))).start()
    drain(qbuf.at[0, 0], qz.at[0])
    passed = qbuf.at[1 - side, x]
    for d in (1, 3, 2):
        remote(passed, passed, qs.at[0], qr.at[1], at(z, turn(x, d))).start()

    def fan_out(g):
        drain(kbuf.at[0, pl.ds(0, 2)], kr.at[g])
        part = kbuf.at[y, pl.ds(2 * g, 2)]
        for d in (1, 3, 2):
            remote(part, part, ys.at[0], yr.at[g], {"qry": turn(y, d)}).start()

    fan_out(0)
    drain(q_ref, lq.at[0])
    drain(e_ref, le.at[0])
    drain(qbuf.at[0, pl.ds(0, NX - 1)], qr.at[0])
    drain(qbuf.at[0, pl.ds(0, NX - 1)], qr.at[1])
    drain(pbuf, pr.at[0])
    end = ebuf[0:1, 0:1]

    def bias_of(g):
        pos = jnp.concatenate([pbuf[2 * g], pbuf[2 * g + 1]], axis=1)
        return jnp.where(pos < end, 0.0, NEG_FILL)

    def scan_pair(g, unused):
        @pl.when(g < 1)
        def _():
            fan_out(g + 1)

        drain(kbuf.at[pl.ds(0, NY - 1), pl.ds(0, 2)], yr.at[g])
        parts = [kbuf[:, 2 * g + j].reshape(keys, width) for j in range(2)]
        bias = bias_of(g)
        for m in range(group):
            qm = qbuf[:, :, :, m * width : (m + 1) * width].reshape(rows, width)
            pieces = []
            for j, part in enumerate(parts):
                s = lax.dot_general(qm, part, (((1,), (1,)), ((), ())), preferred_element_type=jnp.float32)
                sbuf[g, m, :, j * keys : (j + 1) * keys] = s
                t = s + bias[:, j * keys : (j + 1) * keys]
                pieces += [t[:, c * 128 : (c + 1) * 128] for c in range(keys // 128)]
            old = mst[m]
            new = functools.reduce(jnp.maximum, pieces, old)
            total = lst[m] * jnp.exp2((old - new) * to_exp2)
            for piece in pieces:
                total = total + jnp.exp2((piece - new) * to_exp2)
            mst[m] = new
            lst[m] = total
        return unused

    lax.fori_loop(0, 2, scan_pair, 0)

    eye = lax.broadcasted_iota(jnp.int32, (128, 128), 0) == lax.broadcasted_iota(jnp.int32, (128, 128), 1)
    for m in range(group):
        for b in range(rows // 128):
            tops = mst[m, b * 128 : (b + 1) * 128]
            top = jnp.max(tops, axis=1, keepdims=True)
            mass = jnp.sum(lst[m, b * 128 : (b + 1) * 128] * jnp.exp2((tops - top) * to_exp2), axis=1, keepdims=True)
            r = m * (rows // 128) + b
            st[side, x, 0, r : r + 1] = jnp.sum(jnp.where(eye, top, 0.0), axis=0, keepdims=True)
            st[side, x, 1, r : r + 1] = jnp.sum(jnp.where(eye, mass, 0.0), axis=0, keepdims=True)
    own = st.at[side, x]
    for zz in (twin, z):
        for d in (2, 1, 3):
            remote(own, own, ss.at[0], sr.at[0], at(zz, turn(x, d))).start()
    remote(own, own, ss.at[0], sr.at[0], at(twin, x)).start()

    drain(sbuf.at[0, 0, pl.ds(0, 56)], sr.at[0])
    tops = [st[e, i, 0] for e in range(2) for i in range(NX)]
    masses = [st[e, i, 1] for e in range(2) for i in range(NX)]
    top = functools.reduce(jnp.maximum, tops)
    mass = sum(b * jnp.exp2((a - top) * to_exp2) for a, b in zip(tops, masses))
    total = top + jnp.log(mass) * (1.0 / scale)
    for m in range(group):
        for b in range(rows // 128):
            r = m * (rows // 128) + b
            col = jnp.sum(jnp.where(eye, total[r : r + 1], 0.0), axis=1, keepdims=True)
            colb[m, b * 128 : (b + 1) * 128] = jnp.broadcast_to(col, (128, 128))

    def best_pair(g, unused):
        def member(m, acc):
            for r in range(rows // 8):
                col = colb[m, r * 8 : (r + 1) * 8]
                acc = tuple(
                    jnp.maximum(a, sbuf[g, m, r * 8 : (r + 1) * 8, c * 128 : (c + 1) * 128] - col)
                    for c, a in enumerate(acc)
                )
            return acc

        start = tuple(jnp.full((8, 128), NEG_FILL, jnp.float32) for c in range(2 * keys // 128))
        acc = lax.fori_loop(0, group, member, start)
        best = jnp.concatenate([jnp.max(a, axis=0, keepdims=True) for a in acc], axis=1) * scale
        best = jnp.where(bias_of(g) < 0.0, NEG_FILL, best)
        cm[2 * g] = best[:, :keys]
        cm[2 * g + 1] = best[:, keys:]
        return unused

    lax.fori_loop(0, 2, best_pair, 0)

    place = z // 2 * NY + y

    def owner(step, unused):
        far, far_y = turn(slot, step // NY), turn(y, lax.rem(step, NY))
        remote(cm.at[far], rbuf.at[place], cs.at[0], cr.at[0], {"ctx": (HALF * side + far) * NX + x, "qry": far_y}).start()
        return unused

    lax.fori_loop(1, HALF * NY, owner, 0)

    @pl.when(inside)
    def _():
        pltpu.make_async_copy(cm.at[slot], rbuf.at[place], cr.at[0]).start()

    @pl.when(~inside)
    def _():
        owner(0, 0)

    drain(rbuf, cr.at[0])
    o_ref[...] = jnp.max(rbuf[...], axis=0)

    drain(sbuf.at[0, 0, pl.ds(0, 56)], ss.at[0])
    drain(colb.at[pl.ds(0, 7), pl.ds(0, 112)], qs.at[0])
    drain(kbuf.at[pl.ds(0, 3)], ys.at[0])

    @pl.when(inside)
    def _():
        drain(rbuf.at[pl.ds(0, HALF * NY - 1)], cs.at[0])
        drain(kbuf.at[0, pl.ds(0, 3)], ks.at[0])
        drain(pbuf.at[pl.ds(0, 3)], ps.at[0])

    @pl.when(~inside)
    def _():
        drain(rbuf, cs.at[0])
        drain(kbuf.at[0], ks.at[0])
        drain(pbuf, ps.at[0])


def shards(queries, key_cache, key_positions, span_end):
    own, unused, lanes = queries.shape
    keys, width = key_cache.shape[1:]
    group = lanes // width
    rows = own * NX * 2
    dma = lambda n: pltpu.SemaphoreType.DMA((n,))
    return pl.pallas_call(
        functools.partial(kernel, group),
        out_shape=jax.ShapeDtypeStruct((1, keys), jnp.float32),
        in_specs=[pl.BlockSpec(memory_space=pl.ANY)] * 4,
        out_specs=pl.BlockSpec(memory_space=pltpu.VMEM),
        scratch_shapes=[
            pltpu.VMEM((2, NX, own, lanes), jnp.bfloat16),
            pltpu.VMEM((NY, HALF, keys // NY, width), jnp.bfloat16),
            pltpu.VMEM((HALF, 1, keys), jnp.int32),
            pltpu.VMEM((1, own), jnp.int32),
            pltpu.VMEM((2, group, rows, 2 * keys), jnp.float32),
            pltpu.VMEM((group, rows, 128), jnp.float32),
            pltpu.VMEM((group, rows, 128), jnp.float32),
            pltpu.VMEM((group, rows, 128), jnp.float32),
            pltpu.VMEM((2, NX, 2, 16, 128), jnp.float32),
            pltpu.VMEM((HALF, 1, keys), jnp.float32),
            pltpu.VMEM((HALF * NY, 1, keys), jnp.float32),
            dma(1), dma(1), dma(2), dma(1), dma(1), dma(2), dma(1), dma(1), dma(1), dma(2), dma(1), dma(1), dma(1), dma(1), dma(1),
        ],
        compiler_params=pltpu.CompilerParams(collective_id=0, has_side_effects=True, vmem_limit_bytes=58 << 20),
    )(queries[:, 0], key_cache[0], key_positions[None], span_end[None])


def solution(mesh):
    placed = (P(("qry", "ctx"), "head", None), P("head", "ctx", None), P("ctx"), P(("qry", "ctx")))
    return jax.shard_map(shards, mesh=mesh, in_specs=placed, out_specs=P("head", "ctx"), check_vma=False)
```

```python
import functools
import math

import jax
import jax.numpy as jnp
from jax import lax
from jax.experimental import pallas as pl
from jax.experimental.pallas import tpu as pltpu
from jax.sharding import PartitionSpec as P

NEG_FILL = -1e30
MESH = pl.DeviceIdType.MESH
NX, NY, NZ = 4, 4, 8
HALF = NZ // 2


def kernel(group, q_ref, k_ref, p_ref, e_ref, o_ref, qbuf, kbuf, pbuf, ebuf, sbuf, mst, lst, colb, st, cm, rbuf,
           lq, le, qr, qz, qs, kr, pr, ks, ps, yr, ys, ss, sr, cs, cr, ready):
    ctx, y = lax.axis_index("ctx"), lax.axis_index("qry")
    z, x = ctx // NX, lax.rem(ctx, NX)
    side = lax.rem(z, 2)
    twin = z + 1 - 2 * side
    half = z // HALF
    inside = side == half
    keys, width = k_ref.shape
    quarter = keys // NY
    rows = 2 * qbuf.shape[1] * qbuf.shape[2]
    scale = width**-0.5
    to_exp2 = math.log2(math.e) * scale
    mine = pl.ds(pl.multiple_of(y * quarter, quarter), quarter)

    def at(zz, xx):
        return {"ctx": zz * NX + xx}

    def turn(v, d):
        return lax.rem(v + d, 4)

    def remote(src, dst, send, recv, dev):
        return pltpu.make_async_remote_copy(src_ref=src, dst_ref=dst, send_sem=send, recv_sem=recv, device_id=dev, device_id_type=MESH)

    def drain(ref, sem):
        pltpu.make_async_copy(ref, ref, sem).wait()

    barrier = pltpu.get_barrier_semaphore()

    def greet(dev):
        pl.semaphore_signal(barrier, inc=1, device_id=dev, device_id_type=MESH)

    for j in range(HALF):
        source, target = HALF * side + j, 2 * j + half

        @pl.when(source > z)
        def _():
            greet(at(source, x))

        @pl.when(target > z)
        def _():
            greet(at(target, x))

    for v in range(1, 4):

        @pl.when(v > y)
        def _():
            greet({"qry": v})

        @pl.when(v > x)
        def _():
            greet(at(z, v))

    @pl.when(twin > z)
    def _():
        greet(at(twin, x))

    lower = jnp.clip(z - HALF * side, 0, HALF) + (z - half + 1) // 2
    waits = lower + x + y + side

    @pl.when(waits > 0)
    def _():
        pl.semaphore_wait(barrier, waits)


    def tell(index, dev):
        pl.semaphore_signal(ready.at[index], inc=1, device_id=dev, device_id_type=MESH)

    for j in range(HALF):
        source = HALF * side + j

        @pl.when(source < z)
        def _():
            tell(9 + z // 2, at(source, x))

    @pl.when(side == 1)
    def _():
        tell(8, at(twin, x))

    for v in range(3):

        @pl.when(v < x)
        def _():
            tell(x, at(z, v))

        @pl.when(v < y)
        def _():
            tell(4 + y, {"qry": v})

    pltpu.make_async_copy(q_ref, qbuf.at[side, x], lq.at[0]).start()
    pltpu.make_async_copy(e_ref, ebuf, le.at[0]).start()
    slot = lax.rem(z, HALF)

    @pl.when(inside)
    def _():
        pltpu.make_async_copy(k_ref.at[mine], kbuf.at[y, slot], kr.at[slot // 2]).start()
        pltpu.make_async_copy(p_ref, pbuf.at[slot], pr.at[0]).start()

    mst[...] = jnp.full(mst.shape, NEG_FILL, jnp.float32)
    lst[...] = jnp.zeros(lst.shape, jnp.float32)
    st[side, x] = jnp.zeros(st.shape[2:], jnp.float32)
    def send_keys(target):
        remote(k_ref.at[mine], kbuf.at[y, slot], ks.at[0], kr.at[slot // 2], at(target, x)).start()
        remote(p_ref, pbuf.at[slot], ps.at[0], pr.at[0], at(target, x)).start()

    for i in range(HALF):
        target = 2 * i + half

        @pl.when(target < z)
        def _():
            send_keys(target)

    right, left = turn(x, 1), turn(x, 3)

    def send_twin():
        remote(q_ref, qbuf.at[side, x], qs.at[0], qz.at[0], at(twin, x)).start()

    pl.when(side == 1)(send_twin)
    for v in range(NX):
        if v:

            @pl.when(v > x)
            def _():
                pl.semaphore_wait(ready.at[v], 1)

        for index, near in ((0, right), (1, left)):

            @pl.when(v == near)
            def _():
                remote(q_ref, qbuf.at[side, x], qs.at[0], qr.at[index], at(z, v)).start()

    @pl.when(side == 0)
    def _():
        pl.semaphore_wait(ready.at[8], 1)
        send_twin()

    def send_later(near):
        for i in range(HALF):
            target = 2 * i + half

            @pl.when((target > z) & ((target <= z + 2) if near else (target > z + 2)))
            def _():
                pl.semaphore_wait(ready.at[9 + i], 1)
                send_keys(target)

    send_later(True)

    def forward(block, index, device):
        remote(block, block, qs.at[0], qr.at[index], at(z, device)).start()

    drain(q_ref, qr.at[1])
    forward(qbuf.at[side, right], 2, left)
    drain(q_ref, qz.at[0])
    for d in (1, 3, 2):
        forward(qbuf.at[1 - side, x], 3, turn(x, d))
    send_later(False)

    for v in range(1, NY):

        @pl.when(v > y)
        def _():
            pl.semaphore_wait(ready.at[4 + v], 1)

    def fan_out(g):
        drain(kbuf.at[0, pl.ds(0, 2)], kr.at[g])
        part = kbuf.at[y, pl.ds(2 * g, 2)]
        for d in (1, 3, 2):
            remote(part, part, ys.at[0], yr.at[g], {"qry": turn(y, d)}).start()

    flip = jnp.where((z == 4) | (z >= 6), 1, 0)
    fan_out(flip)
    fan_out(1 - flip)
    drain(q_ref, lq.at[0])
    drain(e_ref, le.at[0])
    drain(q_ref, qr.at[0])
    drain(q_ref, qr.at[2])
    drain(qbuf.at[0, pl.ds(0, NX - 1)], qr.at[3])
    drain(pbuf, pr.at[0])
    end = ebuf[0:1, 0:1]

    def bias_of(g):
        pos = jnp.concatenate([pbuf[2 * g], pbuf[2 * g + 1]], axis=1)
        return jnp.where(pos < end, 0.0, NEG_FILL)

    def scan_pair(step, unused):
        g = jnp.where(step == 0, flip, 1 - flip)

        drain(kbuf.at[pl.ds(0, NY - 1), pl.ds(0, 2)], yr.at[g])
        parts = [kbuf[:, 2 * g + j].reshape(keys, width) for j in range(2)]
        bias = bias_of(g)
        for m in range(group):
            qm = qbuf[:, :, :, m * width : (m + 1) * width].reshape(rows, width)
            pieces = []
            for j, part in enumerate(parts):
                s = lax.dot_general(qm, part, (((1,), (1,)), ((), ())), preferred_element_type=jnp.float32)
                sbuf[g, m, :, j * keys : (j + 1) * keys] = s
                t = s + bias[:, j * keys : (j + 1) * keys]
                pieces += [t[:, c * 128 : (c + 1) * 128] for c in range(keys // 128)]
            old = mst[m]
            new = functools.reduce(jnp.maximum, pieces, old)
            total = lst[m] * jnp.exp2((old - new) * to_exp2)
            for piece in pieces:
                total = total + jnp.exp2((piece - new) * to_exp2)
            mst[m] = new
            lst[m] = total
        return unused

    lax.fori_loop(0, 2, scan_pair, 0)

    eye = lax.broadcasted_iota(jnp.int32, (128, 128), 0) == lax.broadcasted_iota(jnp.int32, (128, 128), 1)
    for m in range(group):
        for b in range(rows // 128):
            tops = mst[m, b * 128 : (b + 1) * 128]
            top = jnp.max(tops, axis=1, keepdims=True)
            mass = jnp.sum(lst[m, b * 128 : (b + 1) * 128] * jnp.exp2((tops - top) * to_exp2), axis=1, keepdims=True)
            r = m * (rows // 128) + b
            level = top + jnp.log(mass) * (1.0 / scale)
            st[side, x, r : r + 1] = jnp.sum(jnp.where(eye, level, 0.0), axis=0, keepdims=True)
    own = st.at[side, x]
    for zz in (twin, z):
        for d in (2, 1, 3):
            remote(own, own, ss.at[0], sr.at[0], at(zz, turn(x, d))).start()
    remote(own, own, ss.at[0], sr.at[0], at(twin, x)).start()

    drain(sbuf.at[0, 0, pl.ds(0, 56), pl.ds(0, 256)], sr.at[0])
    levels = [st[e, i] for e in range(2) for i in range(NX)]
    top = functools.reduce(jnp.maximum, levels)
    mass = sum(jnp.exp2((a - top) * to_exp2) for a in levels)
    total = top + jnp.log(mass) * (1.0 / scale)
    for m in range(group):
        for b in range(rows // 128):
            r = m * (rows // 128) + b
            col = jnp.sum(jnp.where(eye, total[r : r + 1], 0.0), axis=1, keepdims=True)
            colb[m, b * 128 : (b + 1) * 128] = jnp.broadcast_to(col, (128, 128))

    def best_pair(g, unused):
        def member(m, acc):
            for r in range(rows // 8):
                col = colb[m, r * 8 : (r + 1) * 8]
                acc = tuple(
                    jnp.maximum(a, sbuf[g, m, r * 8 : (r + 1) * 8, c * 128 : (c + 1) * 128] - col)
                    for c, a in enumerate(acc)
                )
            return acc

        start = tuple(jnp.full((8, 128), NEG_FILL, jnp.float32) for c in range(2 * keys // 128))
        acc = lax.fori_loop(0, group, member, start)
        best = jnp.concatenate([jnp.max(a, axis=0, keepdims=True) for a in acc], axis=1) * scale
        best = jnp.where(bias_of(g) < 0.0, NEG_FILL, best)
        cm[2 * g] = best[:, :keys]
        cm[2 * g + 1] = best[:, keys:]
        return unused

    lax.fori_loop(0, 2, best_pair, 0)

    place = z // 2 * NY + y

    for far in range(HALF):
        owner = HALF * side + far
        for d in range(NY):
            send = lambda: remote(cm.at[far], rbuf.at[place], cs.at[0], cr.at[0], {"ctx": owner * NX + x, "qry": turn(y, d)}).start()
            if d:
                send()
            else:
                pl.when(owner != z)(send)

    @pl.when(inside)
    def _():
        pltpu.make_async_copy(cm.at[slot], rbuf.at[place], cr.at[0]).start()

    drain(rbuf, cr.at[0])
    o_ref[...] = jnp.max(rbuf[...], axis=0)

    drain(sbuf.at[0, 0, pl.ds(0, 56), pl.ds(0, 256)], ss.at[0])
    drain(colb.at[pl.ds(0, 7), pl.ds(0, 112)], qs.at[0])
    drain(kbuf.at[pl.ds(0, 3)], ys.at[0])

    @pl.when(inside)
    def _():
        drain(rbuf.at[pl.ds(0, HALF * NY - 1)], cs.at[0])
        drain(kbuf.at[0, pl.ds(0, 3)], ks.at[0])
        drain(pbuf.at[pl.ds(0, 3)], ps.at[0])

    @pl.when(~inside)
    def _():
        drain(rbuf, cs.at[0])
        drain(kbuf.at[0], ks.at[0])
        drain(pbuf, ps.at[0])


def shards(queries, key_cache, key_positions, span_end):
    own, unused, lanes = queries.shape
    keys, width = key_cache.shape[1:]
    group = lanes // width
    rows = own * NX * 2
    dma = lambda n: pltpu.SemaphoreType.DMA((n,))
    best = pl.pallas_call(
        functools.partial(kernel, group),
        out_shape=jax.ShapeDtypeStruct((1, keys), jnp.float32),
        in_specs=[pl.BlockSpec(memory_space=pl.ANY)] * 4,
        out_specs=pl.BlockSpec(memory_space=pltpu.VMEM),
        scratch_shapes=[
            pltpu.VMEM((2, NX, own, lanes), jnp.bfloat16),
            pltpu.VMEM((NY, HALF, keys // NY, width), jnp.bfloat16),
            pltpu.VMEM((HALF, 1, keys), jnp.int32),
            pltpu.VMEM((1, own), jnp.int32),
            pltpu.VMEM((2, group, rows, 2 * keys), jnp.float32),
            pltpu.VMEM((group, rows, 128), jnp.float32),
            pltpu.VMEM((group, rows, 128), jnp.float32),
            pltpu.VMEM((group, rows, 128), jnp.float32),
            pltpu.VMEM((2, NX, 16, 128), jnp.float32),
            pltpu.VMEM((HALF, 1, keys), jnp.float32),
            pltpu.VMEM((HALF * NY, 1, keys), jnp.float32),
            dma(1), dma(1), dma(4), dma(1), dma(1), dma(2), dma(1), dma(1), dma(1), dma(2), dma(1), dma(1), dma(1), dma(1), dma(1), pltpu.SemaphoreType.REGULAR((13,)),
        ],
        compiler_params=pltpu.CompilerParams(collective_id=0, has_side_effects=True, vmem_limit_bytes=58 << 20),
    )(queries[:, 0], key_cache[0], key_positions[None], span_end[None])
    return best


def solution(mesh):
    placed = (P(("qry", "ctx"), "head", None), P("head", "ctx", None), P("ctx"), P(("qry", "ctx")))
    return jax.shard_map(shards, mesh=mesh, in_specs=placed, out_specs=P("head", "ctx"), check_vma=False)
```

```python
import functools
import math

import jax
import jax.numpy as jnp
from jax import lax
from jax.experimental import pallas as pl
from jax.experimental.pallas import tpu as pltpu
from jax.sharding import PartitionSpec as P

NEG_FILL = -1e30
MESH = pl.DeviceIdType.MESH
NX, NY, NZ = 4, 4, 8
HALF = NZ // 2


def kernel(group, q_ref, k_ref, p_ref, e_ref, o_ref, qbuf, kbuf, pbuf, ebuf, sbuf, mst, lst, colb, st, cm, rbuf,
           lq, le, qr, qz, qs, kr, pr, ks, ps, yr, ys, ss, sr, cs, cr, ready):
    ctx, y = lax.axis_index("ctx"), lax.axis_index("qry")
    z, x = ctx // NX, lax.rem(ctx, NX)
    side = lax.rem(z, 2)
    twin = z + 1 - 2 * side
    half = z // HALF
    inside = side == half
    keys, width = k_ref.shape
    quarter = keys // NY
    rows = 2 * qbuf.shape[1] * qbuf.shape[2]
    scale = width**-0.5
    to_exp2 = math.log2(math.e) * scale
    mine = pl.ds(pl.multiple_of(y * quarter, quarter), quarter)

    def at(zz, xx):
        return {"ctx": zz * NX + xx}

    def turn(v, d):
        return lax.rem(v + d, 4)

    def remote(src, dst, send, recv, dev):
        return pltpu.make_async_remote_copy(src_ref=src, dst_ref=dst, send_sem=send, recv_sem=recv, device_id=dev, device_id_type=MESH)

    def drain(ref, sem):
        pltpu.make_async_copy(ref, ref, sem).wait()

    barrier = pltpu.get_barrier_semaphore()

    def greet(dev):
        pl.semaphore_signal(barrier, inc=1, device_id=dev, device_id_type=MESH)

    for j in range(HALF):
        source, target = HALF * side + j, 2 * j + half

        @pl.when(source > z)
        def _():
            greet(at(source, x))

        @pl.when(target > z)
        def _():
            greet(at(target, x))

    for v in range(1, 4):

        @pl.when(v > y)
        def _():
            greet({"qry": v})

        @pl.when(v > x)
        def _():
            greet(at(z, v))

    @pl.when(twin > z)
    def _():
        greet(at(twin, x))

    lower = jnp.clip(z - HALF * side, 0, HALF) + (z - half + 1) // 2
    waits = lower + x + y + side

    @pl.when(waits > 0)
    def _():
        pl.semaphore_wait(barrier, waits)


    def tell(index, dev):
        pl.semaphore_signal(ready.at[index], inc=1, device_id=dev, device_id_type=MESH)

    for j in range(HALF):
        source = HALF * side + j

        @pl.when(source < z)
        def _():
            tell(9 + z // 2, at(source, x))

    @pl.when(side == 1)
    def _():
        tell(8, at(twin, x))

    for v in range(3):

        @pl.when(v < x)
        def _():
            tell(x, at(z, v))

        @pl.when(v < y)
        def _():
            tell(4 + y, {"qry": v})

    pltpu.make_async_copy(q_ref, qbuf.at[side, x], lq.at[0]).start()
    pltpu.make_async_copy(e_ref, ebuf, le.at[0]).start()
    slot = lax.rem(z, HALF)

    @pl.when(inside)
    def _():
        pltpu.make_async_copy(k_ref.at[mine], kbuf.at[y, slot], kr.at[slot // 2]).start()
        pltpu.make_async_copy(p_ref, pbuf.at[slot], pr.at[0]).start()

    mst[...] = jnp.full(mst.shape, NEG_FILL, jnp.float32)
    lst[...] = jnp.zeros(lst.shape, jnp.float32)
    st[side, x] = jnp.zeros(st.shape[2:], jnp.float32)
    def send_keys(target):
        remote(k_ref.at[mine], kbuf.at[y, slot], ks.at[0], kr.at[slot // 2], at(target, x)).start()
        remote(p_ref, pbuf.at[slot], ps.at[0], pr.at[0], at(target, x)).start()

    for i in range(HALF):
        target = 2 * i + half

        @pl.when(target < z)
        def _():
            send_keys(target)

    right, left = turn(x, 1), turn(x, 3)

    def send_twin():
        remote(q_ref, qbuf.at[side, x], qs.at[0], qz.at[0], at(twin, x)).start()

    pl.when(side == 1)(send_twin)
    for v in range(NX):
        if v:

            @pl.when(v > x)
            def _():
                pl.semaphore_wait(ready.at[v], 1)

        for index, near in ((0, right), (1, left)):

            @pl.when(v == near)
            def _():
                remote(q_ref, qbuf.at[side, x], qs.at[0], qr.at[index], at(z, v)).start()

    @pl.when(side == 0)
    def _():
        pl.semaphore_wait(ready.at[8], 1)
        send_twin()

    def send_later(near):
        for i in range(HALF):
            target = 2 * i + half

            @pl.when((target > z) & ((target <= z + 2) if near else (target > z + 2)))
            def _():
                pl.semaphore_wait(ready.at[9 + i], 1)
                send_keys(target)

    send_later(True)

    def forward(block, index, device):
        remote(block, block, qs.at[0], qr.at[index], at(z, device)).start()

    drain(q_ref, qr.at[1])
    forward(qbuf.at[side, right], 2, left)
    drain(q_ref, qz.at[0])
    for d in (1, 3, 2):
        forward(qbuf.at[1 - side, x], 3, turn(x, d))
    send_later(False)

    for v in range(1, NY):

        @pl.when(v > y)
        def _():
            pl.semaphore_wait(ready.at[4 + v], 1)

    def fan_out(g):
        drain(kbuf.at[0, pl.ds(0, 2)], kr.at[g])
        part = kbuf.at[y, pl.ds(2 * g, 2)]
        for d in (1, 3, 2):
            remote(part, part, ys.at[0], yr.at[g], {"qry": turn(y, d)}).start()

    flip = jnp.where((z == 4) | (z >= 6), 1, 0)
    fan_out(flip)
    fan_out(1 - flip)
    drain(q_ref, lq.at[0])
    drain(e_ref, le.at[0])
    drain(q_ref, qr.at[0])
    drain(q_ref, qr.at[2])
    drain(qbuf.at[0, pl.ds(0, NX - 1)], qr.at[3])
    drain(pbuf, pr.at[0])
    end = ebuf[0:1, 0:1]

    def bias_of(g):
        pos = jnp.concatenate([pbuf[2 * g], pbuf[2 * g + 1]], axis=1)
        return jnp.where(pos < end, 0.0, NEG_FILL)

    def scan_pair(step, unused):
        g = jnp.where(step == 0, flip, 1 - flip)

        drain(kbuf.at[pl.ds(0, NY - 1), pl.ds(0, 2)], yr.at[g])
        parts = [kbuf[:, 2 * g + j].reshape(keys, width) for j in range(2)]
        bias = bias_of(g)
        for m in range(group):
            qm = qbuf[:, :, :, m * width : (m + 1) * width].reshape(rows, width)
            pieces = []
            for j, part in enumerate(parts):
                s = lax.dot_general(qm, part, (((1,), (1,)), ((), ())), preferred_element_type=jnp.float32)
                sbuf[g, m, :, j * keys : (j + 1) * keys] = s
                t = s + bias[:, j * keys : (j + 1) * keys]
                pieces += [t[:, c * 128 : (c + 1) * 128] for c in range(keys // 128)]
            old = mst[m]
            new = functools.reduce(jnp.maximum, pieces, old)
            total = lst[m] * jnp.exp2((old - new) * to_exp2)
            for piece in pieces:
                total = total + jnp.exp2((piece - new) * to_exp2)
            mst[m] = new
            lst[m] = total
        return unused

    lax.fori_loop(0, 2, scan_pair, 0)

    blocks = [(m, b, m * (rows // 128) + b) for m in range(group) for b in range(rows // 128)]
    for m, b, r in blocks:
        tops, masses = mst[m, b * 128 : (b + 1) * 128].T, lst[m, b * 128 : (b + 1) * 128].T
        top = jnp.max(tops, axis=0, keepdims=True)
        mass = jnp.sum(masses * jnp.exp2((tops - top) * to_exp2), axis=0, keepdims=True)
        st[side, x, r : r + 1] = top + jnp.log(mass) * (1.0 / scale)
    own = st.at[side, x]
    for zz in (twin, z):
        for d in (2, 1, 3):
            remote(own, own, ss.at[0], sr.at[0], at(zz, turn(x, d))).start()
    remote(own, own, ss.at[0], sr.at[0], at(twin, x)).start()

    drain(sbuf.at[0, 0, pl.ds(0, 56), pl.ds(0, 256)], sr.at[0])
    levels = [st[e, i] for e in range(2) for i in range(NX)]
    top = functools.reduce(jnp.maximum, levels)
    mass = sum(jnp.exp2((a - top) * to_exp2) for a in levels)
    total = top + jnp.log(mass) * (1.0 / scale)
    for m, b, r in blocks:
        colb[m, b * 128 : (b + 1) * 128] = jnp.broadcast_to(total[r : r + 1], (128, 128)).T

    def best_pair(g, unused):
        def member(m, acc):
            for r in range(rows // 8):
                col = colb[m, r * 8 : (r + 1) * 8]
                acc = tuple(
                    jnp.maximum(a, sbuf[g, m, r * 8 : (r + 1) * 8, c * 128 : (c + 1) * 128] - col)
                    for c, a in enumerate(acc)
                )
            return acc

        start = tuple(jnp.full((8, 128), NEG_FILL, jnp.float32) for c in range(2 * keys // 128))
        acc = lax.fori_loop(0, group, member, start)
        best = jnp.concatenate([jnp.max(a, axis=0, keepdims=True) for a in acc], axis=1) * scale
        best = jnp.where(bias_of(g) < 0.0, NEG_FILL, best)
        cm[2 * g] = best[:, :keys]
        cm[2 * g + 1] = best[:, keys:]
        return unused

    lax.fori_loop(0, 2, best_pair, 0)

    place = z // 2 * NY + y

    for far in range(HALF):
        owner = HALF * side + far
        for d in range(NY):
            send = lambda: remote(cm.at[far], rbuf.at[place], cs.at[0], cr.at[0], {"ctx": owner * NX + x, "qry": turn(y, d)}).start()
            if d:
                send()
            else:
                pl.when(owner != z)(send)

    @pl.when(inside)
    def _():
        pltpu.make_async_copy(cm.at[slot], rbuf.at[place], cr.at[0]).start()

    drain(rbuf, cr.at[0])
    o_ref[...] = jnp.max(rbuf[...], axis=0)

    drain(sbuf.at[0, 0, pl.ds(0, 56), pl.ds(0, 256)], ss.at[0])
    drain(colb.at[pl.ds(0, 7), pl.ds(0, 112)], qs.at[0])
    drain(kbuf.at[pl.ds(0, 3)], ys.at[0])

    @pl.when(inside)
    def _():
        drain(rbuf.at[pl.ds(0, HALF * NY - 1)], cs.at[0])
        drain(kbuf.at[0, pl.ds(0, 3)], ks.at[0])
        drain(pbuf.at[pl.ds(0, 3)], ps.at[0])

    @pl.when(~inside)
    def _():
        drain(rbuf, cs.at[0])
        drain(kbuf.at[0], ks.at[0])
        drain(pbuf, ps.at[0])


def shards(queries, key_cache, key_positions, span_end):
    own, unused, lanes = queries.shape
    keys, width = key_cache.shape[1:]
    group = lanes // width
    rows = own * NX * 2
    dma = lambda n: pltpu.SemaphoreType.DMA((n,))
    best = pl.pallas_call(
        functools.partial(kernel, group),
        out_shape=jax.ShapeDtypeStruct((1, keys), jnp.float32),
        in_specs=[pl.BlockSpec(memory_space=pl.ANY)] * 4,
        out_specs=pl.BlockSpec(memory_space=pltpu.VMEM),
        scratch_shapes=[
            pltpu.VMEM((2, NX, own, lanes), jnp.bfloat16),
            pltpu.VMEM((NY, HALF, keys // NY, width), jnp.bfloat16),
            pltpu.VMEM((HALF, 1, keys), jnp.int32),
            pltpu.VMEM((1, own), jnp.int32),
            pltpu.VMEM((2, group, rows, 2 * keys), jnp.float32),
            pltpu.VMEM((group, rows, 128), jnp.float32),
            pltpu.VMEM((group, rows, 128), jnp.float32),
            pltpu.VMEM((group, rows, 128), jnp.float32),
            pltpu.VMEM((2, NX, 16, 128), jnp.float32),
            pltpu.VMEM((HALF, 1, keys), jnp.float32),
            pltpu.VMEM((HALF * NY, 1, keys), jnp.float32),
            dma(1), dma(1), dma(4), dma(1), dma(1), dma(2), dma(1), dma(1), dma(1), dma(2), dma(1), dma(1), dma(1), dma(1), dma(1), pltpu.SemaphoreType.REGULAR((13,)),
        ],
        compiler_params=pltpu.CompilerParams(collective_id=0, has_side_effects=True, vmem_limit_bytes=58 << 20),
    )(queries[:, 0], key_cache[0], key_positions[None], span_end[None])
    return best


def solution(mesh):
    placed = (P(("qry", "ctx"), "head", None), P("head", "ctx", None), P("ctx"), P(("qry", "ctx")))
    return jax.shard_map(shards, mesh=mesh, in_specs=placed, out_specs=P("head", "ctx"), check_vma=False)
```

```python
import functools
import math

import jax
import jax.numpy as jnp
from jax import lax
from jax.experimental import pallas as pl
from jax.experimental.pallas import tpu as pltpu
from jax.sharding import PartitionSpec as P

NEG_FILL = -1e30
MESH = pl.DeviceIdType.MESH
NX, NY, NZ = 4, 4, 8
HALF = NZ // 2


def kernel(group, q_ref, k_ref, p_ref, e_ref, o_ref, qbuf, kbuf, pbuf, ebuf, sbuf, mst, lst, colb, st, cm, rbuf,
           lq, le, qr, qz, qs, kr, pr, ks, ps, yr, ys, ss, sr, cs, cr, ready):
    ctx, y = lax.axis_index("ctx"), lax.axis_index("qry")
    z, x = ctx // NX, lax.rem(ctx, NX)
    side = lax.rem(z, 2)
    twin = z + 1 - 2 * side
    half = z // HALF
    inside = side == half
    keys, width = k_ref.shape
    quarter = keys // NY
    rows = 2 * qbuf.shape[1] * qbuf.shape[2]
    scale = width**-0.5
    to_exp2 = math.log2(math.e) * scale
    mine = pl.ds(pl.multiple_of(y * quarter, quarter), quarter)

    def at(zz, xx):
        return {"ctx": zz * NX + xx}

    def turn(v, d):
        return lax.rem(v + d, 4)

    def remote(src, dst, send, recv, dev):
        return pltpu.make_async_remote_copy(src_ref=src, dst_ref=dst, send_sem=send, recv_sem=recv, device_id=dev, device_id_type=MESH)

    def drain(ref, sem):
        pltpu.make_async_copy(ref, ref, sem).wait()

    barrier = pltpu.get_barrier_semaphore()

    def greet(dev):
        pl.semaphore_signal(barrier, inc=1, device_id=dev, device_id_type=MESH)

    for j in range(HALF):
        source, target = HALF * side + j, 2 * j + half

        @pl.when(source > z)
        def _():
            greet(at(source, x))

        @pl.when(target > z)
        def _():
            greet(at(target, x))

    for v in range(1, 4):

        @pl.when(v > y)
        def _():
            greet({"qry": v})

        @pl.when(v > x)
        def _():
            greet(at(z, v))

    @pl.when(twin > z)
    def _():
        greet(at(twin, x))

    lower = jnp.clip(z - HALF * side, 0, HALF) + (z - half + 1) // 2
    waits = lower + x + y + side

    @pl.when(waits > 0)
    def _():
        pl.semaphore_wait(barrier, waits)


    def tell(index, dev):
        pl.semaphore_signal(ready.at[index], inc=1, device_id=dev, device_id_type=MESH)

    for j in range(HALF):
        source = HALF * side + j

        @pl.when(source < z)
        def _():
            tell(9 + z // 2, at(source, x))

    @pl.when(side == 1)
    def _():
        tell(8, at(twin, x))

    for v in range(3):

        @pl.when(v < x)
        def _():
            tell(x, at(z, v))

        @pl.when(v < y)
        def _():
            tell(4 + y, {"qry": v})

    pltpu.make_async_copy(q_ref, qbuf.at[side, x], lq.at[0]).start()
    pltpu.make_async_copy(e_ref, ebuf, le.at[0]).start()
    slot = lax.rem(z, HALF)

    @pl.when(inside)
    def _():
        pltpu.make_async_copy(k_ref.at[mine], kbuf.at[y, slot], kr.at[slot // 2]).start()
        pltpu.make_async_copy(p_ref, pbuf.at[slot], pr.at[0]).start()

    def send_keys(target):
        remote(k_ref.at[mine], kbuf.at[y, slot], ks.at[0], kr.at[slot // 2], at(target, x)).start()
        remote(p_ref, pbuf.at[slot], ps.at[0], pr.at[0], at(target, x)).start()

    for i in range(HALF):
        target = 2 * i + half

        @pl.when(target < z)
        def _():
            send_keys(target)

    right, left = turn(x, 1), turn(x, 3)

    def send_twin():
        remote(q_ref, qbuf.at[side, x], qs.at[0], qz.at[0], at(twin, x)).start()

    pl.when(side == 1)(send_twin)
    for v in range(NX):
        if v:

            @pl.when(v > x)
            def _():
                pl.semaphore_wait(ready.at[v], 1)

        for index, near in ((0, right), (1, left)):

            @pl.when(v == near)
            def _():
                remote(q_ref, qbuf.at[side, x], qs.at[0], qr.at[index], at(z, v)).start()

    @pl.when(side == 0)
    def _():
        pl.semaphore_wait(ready.at[8], 1)
        send_twin()

    def send_later(near):
        for i in range(HALF):
            target = 2 * i + half

            @pl.when((target > z) & ((target <= z + 2) if near else (target > z + 2)))
            def _():
                pl.semaphore_wait(ready.at[9 + i], 1)
                send_keys(target)

    send_later(True)

    def forward(block, index, device):
        remote(block, block, qs.at[0], qr.at[index], at(z, device)).start()

    drain(q_ref, qr.at[1])
    forward(qbuf.at[side, right], 2, left)
    drain(q_ref, qz.at[0])
    for d in (1, 3, 2):
        forward(qbuf.at[1 - side, x], 3, turn(x, d))
    send_later(False)

    for v in range(1, NY):

        @pl.when(v > y)
        def _():
            pl.semaphore_wait(ready.at[4 + v], 1)

    def fan_out(g):
        drain(kbuf.at[0, pl.ds(0, 2)], kr.at[g])
        part = kbuf.at[y, pl.ds(2 * g, 2)]
        for d in (1, 3, 2):
            remote(part, part, ys.at[0], yr.at[g], {"qry": turn(y, d)}).start()

    mst[...] = jnp.full(mst.shape, NEG_FILL, jnp.float32)
    lst[...] = jnp.zeros(lst.shape, jnp.float32)
    st[side, x] = jnp.zeros(st.shape[2:], jnp.float32)
    flip = jnp.where((z == 4) | (z >= 6), 1, 0)
    fan_out(flip)
    fan_out(1 - flip)
    drain(q_ref, lq.at[0])
    drain(e_ref, le.at[0])
    drain(q_ref, qr.at[0])
    drain(q_ref, qr.at[2])
    drain(qbuf.at[0, pl.ds(0, NX - 1)], qr.at[3])
    drain(pbuf, pr.at[0])
    end = ebuf[0:1, 0:1]

    def bias_of(g):
        pos = jnp.concatenate([pbuf[2 * g], pbuf[2 * g + 1]], axis=1)
        return jnp.where(pos < end, 0.0, NEG_FILL)

    def scan_pair(step, unused):
        g = jnp.where(step == 0, flip, 1 - flip)

        drain(kbuf.at[pl.ds(0, NY - 1), pl.ds(0, 2)], yr.at[g])
        parts = [kbuf[:, 2 * g + j].reshape(keys, width) for j in range(2)]
        bias = bias_of(g)
        for m in range(group):
            qm = qbuf[:, :, :, m * width : (m + 1) * width].reshape(rows, width)
            pieces = []
            for j, part in enumerate(parts):
                s = lax.dot_general(qm, part, (((1,), (1,)), ((), ())), preferred_element_type=jnp.float32)
                sbuf[g, m, :, j * keys : (j + 1) * keys] = s
                t = s + bias[:, j * keys : (j + 1) * keys]
                pieces += [t[:, c * 128 : (c + 1) * 128] for c in range(keys // 128)]
            old = mst[m]
            new = functools.reduce(jnp.maximum, pieces, old)
            total = lst[m] * jnp.exp2((old - new) * to_exp2)
            for piece in pieces:
                total = total + jnp.exp2((piece - new) * to_exp2)
            mst[m] = new
            lst[m] = total
        return unused

    lax.fori_loop(0, 2, scan_pair, 0)

    blocks = [(m, b, m * (rows // 128) + b) for m in range(group) for b in range(rows // 128)]
    for m, b, r in blocks:
        tops, masses = mst[m, b * 128 : (b + 1) * 128].T, lst[m, b * 128 : (b + 1) * 128].T
        top = jnp.max(tops, axis=0, keepdims=True)
        mass = jnp.sum(masses * jnp.exp2((tops - top) * to_exp2), axis=0, keepdims=True)
        st[side, x, r : r + 1] = top + jnp.log(mass) * (1.0 / scale)
    own = st.at[side, x]
    for zz in (twin, z):
        for d in (2, 1, 3):
            remote(own, own, ss.at[0], sr.at[0], at(zz, turn(x, d))).start()
    remote(own, own, ss.at[0], sr.at[0], at(twin, x)).start()

    drain(sbuf.at[0, 0, pl.ds(0, 56), pl.ds(0, 256)], sr.at[0])
    levels = [st[e, i] for e in range(2) for i in range(NX)]
    top = functools.reduce(jnp.maximum, levels)
    mass = sum(jnp.exp2((a - top) * to_exp2) for a in levels)
    total = top + jnp.log(mass) * (1.0 / scale)
    for m, b, r in blocks:
        colb[m, b * 128 : (b + 1) * 128] = jnp.broadcast_to(total[r : r + 1], (128, 128)).T

    place = z // 2 * NY + y

    def best_pair(g, unused):
        def member(m, acc):
            for r in range(rows // 8):
                col = colb[m, r * 8 : (r + 1) * 8]
                acc = tuple(
                    jnp.maximum(a, sbuf[g, m, r * 8 : (r + 1) * 8, c * 128 : (c + 1) * 128] - col)
                    for c, a in enumerate(acc)
                )
            return acc

        start = tuple(jnp.full((8, 128), NEG_FILL, jnp.float32) for c in range(2 * keys // 128))
        acc = lax.fori_loop(0, group, member, start)
        best = jnp.concatenate([jnp.max(a, axis=0, keepdims=True) for a in acc], axis=1) * scale
        best = jnp.where(bias_of(g) < 0.0, NEG_FILL, best)
        cm[2 * g] = best[:, :keys]
        cm[2 * g + 1] = best[:, keys:]
        for j in range(2):
            far = 2 * g + j
            owner = HALF * side + far
            for d in range(NY):
                send = lambda: remote(cm.at[far], rbuf.at[place], cs.at[0], cr.at[0], {"ctx": owner * NX + x, "qry": turn(y, d)}).start()
                if d:
                    send()
                else:
                    pl.when(owner != z)(send)
        return unused

    lax.fori_loop(0, 2, best_pair, 0)


    @pl.when(inside)
    def _():
        pltpu.make_async_copy(cm.at[slot], rbuf.at[place], cr.at[0]).start()

    drain(rbuf, cr.at[0])
    o_ref[...] = jnp.max(rbuf[...], axis=0)

    drain(sbuf.at[0, 0, pl.ds(0, 56), pl.ds(0, 256)], ss.at[0])
    drain(colb.at[pl.ds(0, 7), pl.ds(0, 112)], qs.at[0])
    drain(kbuf.at[pl.ds(0, 3)], ys.at[0])

    @pl.when(inside)
    def _():
        drain(rbuf.at[pl.ds(0, HALF * NY - 1)], cs.at[0])
        drain(kbuf.at[0, pl.ds(0, 3)], ks.at[0])
        drain(pbuf.at[pl.ds(0, 3)], ps.at[0])

    @pl.when(~inside)
    def _():
        drain(rbuf, cs.at[0])
        drain(kbuf.at[0], ks.at[0])
        drain(pbuf, ps.at[0])


def shards(queries, key_cache, key_positions, span_end):
    own, unused, lanes = queries.shape
    keys, width = key_cache.shape[1:]
    group = lanes // width
    rows = own * NX * 2
    dma = lambda n: pltpu.SemaphoreType.DMA((n,))
    best = pl.pallas_call(
        functools.partial(kernel, group),
        out_shape=jax.ShapeDtypeStruct((1, keys), jnp.float32),
        in_specs=[pl.BlockSpec(memory_space=pl.ANY)] * 4,
        out_specs=pl.BlockSpec(memory_space=pltpu.VMEM),
        scratch_shapes=[
            pltpu.VMEM((2, NX, own, lanes), jnp.bfloat16),
            pltpu.VMEM((NY, HALF, keys // NY, width), jnp.bfloat16),
            pltpu.VMEM((HALF, 1, keys), jnp.int32),
            pltpu.VMEM((1, own), jnp.int32),
            pltpu.VMEM((2, group, rows, 2 * keys), jnp.float32),
            pltpu.VMEM((group, rows, 128), jnp.float32),
            pltpu.VMEM((group, rows, 128), jnp.float32),
            pltpu.VMEM((group, rows, 128), jnp.float32),
            pltpu.VMEM((2, NX, 16, 128), jnp.float32),
            pltpu.VMEM((HALF, 1, keys), jnp.float32),
            pltpu.VMEM((HALF * NY, 1, keys), jnp.float32),
            dma(1), dma(1), dma(4), dma(1), dma(1), dma(2), dma(1), dma(1), dma(1), dma(2), dma(1), dma(1), dma(1), dma(1), dma(1), pltpu.SemaphoreType.REGULAR((13,)),
        ],
        compiler_params=pltpu.CompilerParams(collective_id=0, has_side_effects=True, vmem_limit_bytes=58 << 20),
    )(queries[:, 0], key_cache[0], key_positions[None], span_end[None])
    return best


def solution(mesh):
    placed = (P(("qry", "ctx"), "head", None), P("head", "ctx", None), P("ctx"), P(("qry", "ctx")))
    return jax.shard_map(shards, mesh=mesh, in_specs=placed, out_specs=P("head", "ctx"), check_vma=False)
```

```python
import functools
import math

import jax
import jax.numpy as jnp
from jax import lax
from jax.experimental import pallas as pl
from jax.experimental.pallas import tpu as pltpu
from jax.sharding import PartitionSpec as P

NEG_FILL = -1e30
MESH = pl.DeviceIdType.MESH
NX, NY, NZ = 4, 4, 8
HALF = NZ // 2


def kernel(group, q_ref, k_ref, p_ref, e_ref, o_ref, qbuf, kbuf, pbuf, ebuf, sbuf, mst, lst, colb, st, cm, rbuf, kown,
           lk, lq, le, qr, qz, qs, kr, pr, ks, ps, yr, ys, ss, sr, cs, cr, ready):
    ctx, y = lax.axis_index("ctx"), lax.axis_index("qry")
    z, x = ctx // NX, lax.rem(ctx, NX)
    side = lax.rem(z, 2)
    twin = z + 1 - 2 * side
    half = z // HALF
    inside = side == half
    keys, width = k_ref.shape
    quarter = keys // NY
    rows = 2 * qbuf.shape[1] * qbuf.shape[2]
    scale = width**-0.5
    to_exp2 = math.log2(math.e) * scale
    mine = pl.ds(pl.multiple_of(y * quarter, quarter), quarter)

    def at(zz, xx):
        return {"ctx": zz * NX + xx}

    def turn(v, d):
        return lax.rem(v + d, 4)

    def remote(src, dst, send, recv, dev):
        return pltpu.make_async_remote_copy(src_ref=src, dst_ref=dst, send_sem=send, recv_sem=recv, device_id=dev, device_id_type=MESH)

    def drain(ref, sem):
        pltpu.make_async_copy(ref, ref, sem).wait()

    barrier = pltpu.get_barrier_semaphore()

    def greet(dev):
        pl.semaphore_signal(barrier, inc=1, device_id=dev, device_id_type=MESH)

    for j in range(HALF):
        source, target = HALF * side + j, 2 * j + half

        @pl.when(source > z)
        def _():
            greet(at(source, x))

        @pl.when(target > z)
        def _():
            greet(at(target, x))

    for v in range(1, 4):

        @pl.when(v > y)
        def _():
            greet({"qry": v})

        @pl.when(v > x)
        def _():
            greet(at(z, v))

    @pl.when(twin > z)
    def _():
        greet(at(twin, x))

    lower = jnp.clip(z - HALF * side, 0, HALF) + (z - half + 1) // 2
    waits = lower + x + y + side

    @pl.when(waits > 0)
    def _():
        pl.semaphore_wait(barrier, waits)


    def tell(index, dev):
        pl.semaphore_signal(ready.at[index], inc=1, device_id=dev, device_id_type=MESH)

    for j in range(HALF):
        source = HALF * side + j

        @pl.when(source < z)
        def _():
            tell(9 + z // 2, at(source, x))

    @pl.when(side == 1)
    def _():
        tell(8, at(twin, x))

    for v in range(3):

        @pl.when(v < x)
        def _():
            tell(x, at(z, v))

        @pl.when(v < y)
        def _():
            tell(4 + y, {"qry": v})

    pltpu.make_async_copy(q_ref, qbuf.at[side, x], lq.at[0]).start()
    pltpu.make_async_copy(e_ref, ebuf, le.at[0]).start()
    pltpu.make_async_copy(k_ref.at[mine], kown, lk.at[0]).start()
    slot = lax.rem(z, HALF)

    @pl.when(inside)
    def _():
        pltpu.make_async_copy(k_ref.at[mine], kbuf.at[y, slot], kr.at[slot // 2]).start()
        pltpu.make_async_copy(p_ref, pbuf.at[slot], pr.at[0]).start()

    def send_keys(target, block):
        remote(block, kbuf.at[y, slot], ks.at[0], kr.at[slot // 2], at(target, x)).start()
        remote(p_ref, pbuf.at[slot], ps.at[0], pr.at[0], at(target, x)).start()

    for i in range(HALF):
        target = 2 * i + half

        @pl.when(target < z)
        def _():
            send_keys(target, k_ref.at[mine])

    right, left = turn(x, 1), turn(x, 3)

    def send_twin():
        remote(q_ref, qbuf.at[side, x], qs.at[0], qz.at[0], at(twin, x)).start()

    pl.when(side == 1)(send_twin)
    for v in range(NX):
        if v:

            @pl.when(v > x)
            def _():
                pl.semaphore_wait(ready.at[v], 1)

        for index, near in ((0, right), (1, left)):

            @pl.when(v == near)
            def _():
                remote(q_ref, qbuf.at[side, x], qs.at[0], qr.at[index], at(z, v)).start()

    @pl.when(side == 0)
    def _():
        pl.semaphore_wait(ready.at[8], 1)
        send_twin()

    def send_later(near):
        for i in range(HALF):
            target = 2 * i + half

            @pl.when((target > z) & ((target <= z + 2) if near else (target > z + 2)))
            def _():
                pl.semaphore_wait(ready.at[9 + i], 1)
                send_keys(target, kown)

    drain(kown, lk.at[0])
    send_later(True)

    def forward(block, index, device):
        remote(block, block, qs.at[0], qr.at[index], at(z, device)).start()

    drain(q_ref, qr.at[1])
    forward(qbuf.at[side, right], 2, left)
    drain(q_ref, qz.at[0])
    for d in (1, 3, 2):
        forward(qbuf.at[1 - side, x], 3, turn(x, d))
    send_later(False)

    for v in range(1, NY):

        @pl.when(v > y)
        def _():
            pl.semaphore_wait(ready.at[4 + v], 1)

    def fan_out(g):
        drain(kbuf.at[0, pl.ds(0, 2)], kr.at[g])
        part = kbuf.at[y, pl.ds(2 * g, 2)]
        for d in (1, 3, 2):
            remote(part, part, ys.at[0], yr.at[g], {"qry": turn(y, d)}).start()

    mst[...] = jnp.full(mst.shape, NEG_FILL, jnp.float32)
    lst[...] = jnp.zeros(lst.shape, jnp.float32)
    st[side, x] = jnp.zeros(st.shape[2:], jnp.float32)
    flip = jnp.where((z == 4) | (z >= 6), 1, 0)
    fan_out(flip)
    fan_out(1 - flip)
    drain(q_ref, lq.at[0])
    drain(e_ref, le.at[0])
    drain(q_ref, qr.at[0])
    drain(q_ref, qr.at[2])
    drain(qbuf.at[0, pl.ds(0, NX - 1)], qr.at[3])
    drain(pbuf, pr.at[0])
    end = ebuf[0:1, 0:1]

    def bias_of(g):
        pos = jnp.concatenate([pbuf[2 * g], pbuf[2 * g + 1]], axis=1)
        return jnp.where(pos < end, 0.0, NEG_FILL)

    def scan_pair(step, unused):
        g = jnp.where(step == 0, flip, 1 - flip)

        drain(kbuf.at[pl.ds(0, NY - 1), pl.ds(0, 2)], yr.at[g])
        parts = [kbuf[:, 2 * g + j].reshape(keys, width) for j in range(2)]
        bias = bias_of(g)
        for m in range(group):
            qm = qbuf[:, :, :, m * width : (m + 1) * width].reshape(rows, width)
            pieces = []
            for j, part in enumerate(parts):
                s = lax.dot_general(qm, part, (((1,), (1,)), ((), ())), preferred_element_type=jnp.float32)
                sbuf[g, m, :, j * keys : (j + 1) * keys] = s
                t = s + bias[:, j * keys : (j + 1) * keys]
                pieces += [t[:, c * 128 : (c + 1) * 128] for c in range(keys // 128)]
            old = mst[m]
            new = functools.reduce(jnp.maximum, pieces, old)
            total = lst[m] * jnp.exp2((old - new) * to_exp2)
            for piece in pieces:
                total = total + jnp.exp2((piece - new) * to_exp2)
            mst[m] = new
            lst[m] = total
        return unused

    lax.fori_loop(0, 2, scan_pair, 0)

    blocks = [(m, b, m * (rows // 128) + b) for m in range(group) for b in range(rows // 128)]
    for m, b, r in blocks:
        tops, masses = mst[m, b * 128 : (b + 1) * 128].T, lst[m, b * 128 : (b + 1) * 128].T
        top = jnp.max(tops, axis=0, keepdims=True)
        mass = jnp.sum(masses * jnp.exp2((tops - top) * to_exp2), axis=0, keepdims=True)
        st[side, x, r : r + 1] = top + jnp.log(mass) * (1.0 / scale)
    own = st.at[side, x]
    for zz in (twin, z):
        for d in (2, 1, 3):
            remote(own, own, ss.at[0], sr.at[0], at(zz, turn(x, d))).start()
    remote(own, own, ss.at[0], sr.at[0], at(twin, x)).start()

    drain(sbuf.at[0, 0, pl.ds(0, 56), pl.ds(0, 256)], sr.at[0])
    levels = [st[e, i] for e in range(2) for i in range(NX)]
    top = functools.reduce(jnp.maximum, levels)
    mass = sum(jnp.exp2((a - top) * to_exp2) for a in levels)
    total = top + jnp.log(mass) * (1.0 / scale)
    for m, b, r in blocks:
        colb[m, b * 128 : (b + 1) * 128] = jnp.broadcast_to(total[r : r + 1], (128, 128)).T

    place = z // 2 * NY + y

    def best_pair(g, unused):
        def member(m, acc):
            for r in range(rows // 8):
                col = colb[m, r * 8 : (r + 1) * 8]
                acc = tuple(
                    jnp.maximum(a, sbuf[g, m, r * 8 : (r + 1) * 8, c * 128 : (c + 1) * 128] - col)
                    for c, a in enumerate(acc)
                )
            return acc

        start = tuple(jnp.full((8, 128), NEG_FILL, jnp.float32) for c in range(2 * keys // 128))
        acc = lax.fori_loop(0, group, member, start)
        best = jnp.concatenate([jnp.max(a, axis=0, keepdims=True) for a in acc], axis=1) * scale
        best = jnp.where(bias_of(g) < 0.0, NEG_FILL, best)
        cm[2 * g] = best[:, :keys]
        cm[2 * g + 1] = best[:, keys:]
        for j in range(2):
            far = 2 * g + j
            owner = HALF * side + far
            for d in range(NY):
                send = lambda: remote(cm.at[far], rbuf.at[place], cs.at[0], cr.at[0], {"ctx": owner * NX + x, "qry": turn(y, d)}).start()
                if d:
                    send()
                else:
                    pl.when(owner != z)(send)
        return unused

    lax.fori_loop(0, 2, best_pair, 0)


    @pl.when(inside)
    def _():
        pltpu.make_async_copy(cm.at[slot], rbuf.at[place], cr.at[0]).start()

    drain(rbuf, cr.at[0])
    o_ref[...] = jnp.max(rbuf[...], axis=0)

    drain(sbuf.at[0, 0, pl.ds(0, 56), pl.ds(0, 256)], ss.at[0])
    drain(colb.at[pl.ds(0, 7), pl.ds(0, 112)], qs.at[0])
    drain(kbuf.at[pl.ds(0, 3)], ys.at[0])

    @pl.when(inside)
    def _():
        drain(rbuf.at[pl.ds(0, HALF * NY - 1)], cs.at[0])
        drain(kbuf.at[0, pl.ds(0, 3)], ks.at[0])
        drain(pbuf.at[pl.ds(0, 3)], ps.at[0])

    @pl.when(~inside)
    def _():
        drain(rbuf, cs.at[0])
        drain(kbuf.at[0], ks.at[0])
        drain(pbuf, ps.at[0])


def shards(queries, key_cache, key_positions, span_end):
    own, unused, lanes = queries.shape
    keys, width = key_cache.shape[1:]
    group = lanes // width
    rows = own * NX * 2
    dma = lambda n: pltpu.SemaphoreType.DMA((n,))
    best = pl.pallas_call(
        functools.partial(kernel, group),
        out_shape=jax.ShapeDtypeStruct((1, keys), jnp.float32),
        in_specs=[pl.BlockSpec(memory_space=pl.ANY)] * 4,
        out_specs=pl.BlockSpec(memory_space=pltpu.VMEM),
        scratch_shapes=[
            pltpu.VMEM((2, NX, own, lanes), jnp.bfloat16),
            pltpu.VMEM((NY, HALF, keys // NY, width), jnp.bfloat16),
            pltpu.VMEM((HALF, 1, keys), jnp.int32),
            pltpu.VMEM((1, own), jnp.int32),
            pltpu.VMEM((2, group, rows, 2 * keys), jnp.float32),
            pltpu.VMEM((group, rows, 128), jnp.float32),
            pltpu.VMEM((group, rows, 128), jnp.float32),
            pltpu.VMEM((group, rows, 128), jnp.float32),
            pltpu.VMEM((2, NX, 16, 128), jnp.float32),
            pltpu.VMEM((HALF, 1, keys), jnp.float32),
            pltpu.VMEM((HALF * NY, 1, keys), jnp.float32),
            pltpu.VMEM((keys // NY, width), jnp.bfloat16),
            dma(1), dma(1), dma(1), dma(4), dma(1), dma(1), dma(2), dma(1), dma(1), dma(1), dma(2), dma(1), dma(1), dma(1), dma(1), dma(1), pltpu.SemaphoreType.REGULAR((13,)),
        ],
        compiler_params=pltpu.CompilerParams(collective_id=0, has_side_effects=True, vmem_limit_bytes=58 << 20),
    )(queries[:, 0], key_cache[0], key_positions[None], span_end[None])
    return best


def solution(mesh):
    placed = (P(("qry", "ctx"), "head", None), P("head", "ctx", None), P("ctx"), P(("qry", "ctx")))
    return jax.shard_map(shards, mesh=mesh, in_specs=placed, out_specs=P("head", "ctx"), check_vma=False)
```

```python
import functools
import math

import jax
import jax.numpy as jnp
from jax import lax
from jax.experimental import pallas as pl
from jax.experimental.pallas import tpu as pltpu
from jax.sharding import PartitionSpec as P

NEG_FILL = -1e30
MESH = pl.DeviceIdType.MESH
NX, NY, NZ = 4, 4, 8
HALF = NZ // 2


def kernel(group, q_ref, k_ref, p_ref, e_ref, o_ref, qbuf, kbuf, pbuf, ebuf, sbuf, mst, lst, colb, st, cm, rbuf, kown,
           lk, lq, le, qr, qz, qs, kr, pr, ks, ps, yr, ys, ss, sr, cs, cr, ready):
    ctx, y = lax.axis_index("ctx"), lax.axis_index("qry")
    z, x = ctx // NX, lax.rem(ctx, NX)
    side = lax.rem(z, 2)
    twin = z + 1 - 2 * side
    half = z // HALF
    inside = side == half
    keys, width = k_ref.shape
    quarter = keys // NY
    rows = 2 * qbuf.shape[1] * qbuf.shape[2]
    scale = width**-0.5
    to_exp2 = math.log2(math.e) * scale
    mine = pl.ds(pl.multiple_of(y * quarter, quarter), quarter)

    def at(zz, xx):
        return {"ctx": zz * NX + xx}

    def turn(v, d):
        return lax.rem(v + d, 4)

    def remote(src, dst, send, recv, dev):
        return pltpu.make_async_remote_copy(src_ref=src, dst_ref=dst, send_sem=send, recv_sem=recv, device_id=dev, device_id_type=MESH)

    def drain(ref, sem):
        pltpu.make_async_copy(ref, ref, sem).wait()

    barrier = pltpu.get_barrier_semaphore()

    def greet(dev):
        pl.semaphore_signal(barrier, inc=1, device_id=dev, device_id_type=MESH)

    for j in range(HALF):
        source, target = HALF * side + j, 2 * j + half

        @pl.when(source > z)
        def _():
            greet(at(source, x))

        @pl.when(target > z)
        def _():
            greet(at(target, x))

    for v in range(1, 4):

        @pl.when(v > y)
        def _():
            greet({"qry": v})

        @pl.when(v > x)
        def _():
            greet(at(z, v))

    @pl.when(twin > z)
    def _():
        greet(at(twin, x))

    lower = jnp.clip(z - HALF * side, 0, HALF) + (z - half + 1) // 2
    waits = lower + x + y + side

    @pl.when(waits > 0)
    def _():
        pl.semaphore_wait(barrier, waits)


    def tell(index, dev):
        pl.semaphore_signal(ready.at[index], inc=1, device_id=dev, device_id_type=MESH)

    for j in range(HALF):
        source = HALF * side + j

        @pl.when(source < z)
        def _():
            tell(9 + z // 2, at(source, x))

    @pl.when(side == 1)
    def _():
        tell(8, at(twin, x))

    for v in range(3):

        @pl.when(v < x)
        def _():
            tell(x, at(z, v))

        @pl.when(v < y)
        def _():
            tell(4 + y, {"qry": v})

    pltpu.make_async_copy(q_ref, qbuf.at[side, x], lq.at[0]).start()
    pltpu.make_async_copy(e_ref, ebuf, le.at[0]).start()
    pltpu.make_async_copy(k_ref.at[mine], kown, lk.at[0]).start()
    slot = lax.rem(z, HALF)

    @pl.when(inside)
    def _():
        pltpu.make_async_copy(k_ref.at[mine], kbuf.at[y, slot], kr.at[slot // 2]).start()
        pltpu.make_async_copy(p_ref, pbuf.at[slot], pr.at[0]).start()

    def send_keys(target, block):
        remote(block, kbuf.at[y, slot], ks.at[0], kr.at[slot // 2], at(target, x)).start()
        remote(p_ref, pbuf.at[slot], ps.at[0], pr.at[0], at(target, x)).start()

    for i in range(HALF):
        target = 2 * i + half

        @pl.when(target < z)
        def _():
            send_keys(target, k_ref.at[mine])

    right, left = turn(x, 1), turn(x, 3)

    def send_twin():
        remote(q_ref, qbuf.at[side, x], qs.at[0], qz.at[0], at(twin, x)).start()

    pl.when(side == 1)(send_twin)
    for v in range(NX):
        if v:

            @pl.when(v > x)
            def _():
                pl.semaphore_wait(ready.at[v], 1)

        for index, near in ((0, right), (1, left)):

            @pl.when(v == near)
            def _():
                remote(q_ref, qbuf.at[side, x], qs.at[0], qr.at[index], at(z, v)).start()

    @pl.when(side == 0)
    def _():
        pl.semaphore_wait(ready.at[8], 1)
        send_twin()

    def send_later(near):
        for i in range(HALF):
            target = 2 * i + half

            @pl.when((target > z) & ((target <= z + 2) if near else (target > z + 2)))
            def _():
                pl.semaphore_wait(ready.at[9 + i], 1)
                send_keys(target, kown)

    drain(kown, lk.at[0])
    send_later(True)

    def forward(block, index, device):
        remote(block, block, qs.at[0], qr.at[index], at(z, device)).start()

    drain(q_ref, qr.at[1])
    forward(qbuf.at[side, right], 2, left)
    drain(q_ref, qz.at[0])
    for d in (1, 3, 2):
        forward(qbuf.at[1 - side, x], 3, turn(x, d))
    send_later(False)

    for v in range(1, NY):

        @pl.when(v > y)
        def _():
            pl.semaphore_wait(ready.at[4 + v], 1)

    def fan_out(g):
        drain(kbuf.at[0, pl.ds(0, 2)], kr.at[g])
        part = kbuf.at[y, pl.ds(2 * g, 2)]
        for d in (1, 3, 2):
            remote(part, part, ys.at[0], yr.at[g], {"qry": turn(y, d)}).start()

    st[side, x] = jnp.zeros(st.shape[2:], jnp.float32)
    flip = jnp.where((z == 4) | (z >= 6), 1, 0)
    fan_out(flip)
    fan_out(1 - flip)
    drain(q_ref, lq.at[0])
    drain(e_ref, le.at[0])
    drain(q_ref, qr.at[0])
    drain(q_ref, qr.at[2])
    drain(qbuf.at[0, pl.ds(0, NX - 1)], qr.at[3])
    drain(pbuf, pr.at[0])
    end = ebuf[0:1, 0:1]

    def bias_of(g):
        pos = jnp.concatenate([pbuf[2 * g], pbuf[2 * g + 1]], axis=1)
        return jnp.where(pos < end, 0.0, NEG_FILL)

    def scan_pair(step):
        g = 1 - flip if step else flip

        drain(kbuf.at[pl.ds(0, NY - 1), pl.ds(0, 2)], yr.at[g])
        parts = [kbuf[:, 2 * g + j].reshape(keys, width) for j in range(2)]
        bias = bias_of(g)
        for m in range(group):
            qm = qbuf[:, :, :, m * width : (m + 1) * width].reshape(rows, width)
            pieces = []
            for j, part in enumerate(parts):
                s = lax.dot_general(qm, part, (((1,), (1,)), ((), ())), preferred_element_type=jnp.float32)
                sbuf[g, m, :, j * keys : (j + 1) * keys] = s
                t = s + bias[:, j * keys : (j + 1) * keys]
                pieces += [t[:, c * 128 : (c + 1) * 128] for c in range(keys // 128)]
            if step:
                new = functools.reduce(jnp.maximum, pieces, mst[m])
                total = lst[m] * jnp.exp2((mst[m] - new) * to_exp2)
            else:
                new = functools.reduce(jnp.maximum, pieces)
                total = jnp.zeros_like(new)
            for piece in pieces:
                total = total + jnp.exp2((piece - new) * to_exp2)
            mst[m] = new
            lst[m] = total

    for step in range(2):
        scan_pair(step)

    blocks = [(m, b, m * (rows // 128) + b) for m in range(group) for b in range(rows // 128)]
    for m, b, r in blocks:
        tops, masses = mst[m, b * 128 : (b + 1) * 128].T, lst[m, b * 128 : (b + 1) * 128].T
        top = jnp.max(tops, axis=0, keepdims=True)
        mass = jnp.sum(masses * jnp.exp2((tops - top) * to_exp2), axis=0, keepdims=True)
        st[side, x, r : r + 1] = top + jnp.log(mass) * (1.0 / scale)
    own = st.at[side, x]
    for zz in (twin, z):
        for d in (2, 1, 3):
            remote(own, own, ss.at[0], sr.at[0], at(zz, turn(x, d))).start()
    remote(own, own, ss.at[0], sr.at[0], at(twin, x)).start()

    drain(sbuf.at[0, 0, pl.ds(0, 56), pl.ds(0, 256)], sr.at[0])
    levels = [st[e, i] for e in range(2) for i in range(NX)]
    top = functools.reduce(jnp.maximum, levels)
    mass = sum(jnp.exp2((a - top) * to_exp2) for a in levels)
    total = top + jnp.log(mass) * (1.0 / scale)
    for m, b, r in blocks:
        colb[m, b * 128 : (b + 1) * 128] = jnp.broadcast_to(total[r : r + 1], (128, 128)).T

    place = z // 2 * NY + y

    def best_pair(g, unused):
        def member(m, acc):
            for r in range(rows // 8):
                col = colb[m, r * 8 : (r + 1) * 8]
                acc = tuple(
                    jnp.maximum(a, sbuf[g, m, r * 8 : (r + 1) * 8, c * 128 : (c + 1) * 128] - col)
                    for c, a in enumerate(acc)
                )
            return acc

        start = tuple(jnp.full((8, 128), NEG_FILL, jnp.float32) for c in range(2 * keys // 128))
        acc = lax.fori_loop(0, group, member, start)
        best = jnp.concatenate([jnp.max(a, axis=0, keepdims=True) for a in acc], axis=1) * scale
        best = jnp.where(bias_of(g) < 0.0, NEG_FILL, best)
        cm[2 * g] = best[:, :keys]
        cm[2 * g + 1] = best[:, keys:]
        for j in range(2):
            far = 2 * g + j
            owner = HALF * side + far
            for d in range(NY):
                send = lambda: remote(cm.at[far], rbuf.at[place], cs.at[0], cr.at[0], {"ctx": owner * NX + x, "qry": turn(y, d)}).start()
                if d:
                    send()
                else:
                    pl.when(owner != z)(send)
        return unused

    lax.fori_loop(0, 2, best_pair, 0)


    @pl.when(inside)
    def _():
        pltpu.make_async_copy(cm.at[slot], rbuf.at[place], cr.at[0]).start()

    drain(rbuf, cr.at[0])
    o_ref[...] = jnp.max(rbuf[...], axis=0)

    drain(sbuf.at[0, 0, pl.ds(0, 56), pl.ds(0, 256)], ss.at[0])
    drain(colb.at[pl.ds(0, 7), pl.ds(0, 112)], qs.at[0])
    drain(kbuf.at[pl.ds(0, 3)], ys.at[0])

    @pl.when(inside)
    def _():
        drain(rbuf.at[pl.ds(0, HALF * NY - 1)], cs.at[0])
        drain(kbuf.at[0, pl.ds(0, 3)], ks.at[0])
        drain(pbuf.at[pl.ds(0, 3)], ps.at[0])

    @pl.when(~inside)
    def _():
        drain(rbuf, cs.at[0])
        drain(kbuf.at[0], ks.at[0])
        drain(pbuf, ps.at[0])


def shards(queries, key_cache, key_positions, span_end):
    own, unused, lanes = queries.shape
    keys, width = key_cache.shape[1:]
    group = lanes // width
    rows = own * NX * 2
    dma = lambda n: pltpu.SemaphoreType.DMA((n,))
    best = pl.pallas_call(
        functools.partial(kernel, group),
        out_shape=jax.ShapeDtypeStruct((1, keys), jnp.float32),
        in_specs=[pl.BlockSpec(memory_space=pl.ANY)] * 4,
        out_specs=pl.BlockSpec(memory_space=pltpu.VMEM),
        scratch_shapes=[
            pltpu.VMEM((2, NX, own, lanes), jnp.bfloat16),
            pltpu.VMEM((NY, HALF, keys // NY, width), jnp.bfloat16),
            pltpu.VMEM((HALF, 1, keys), jnp.int32),
            pltpu.VMEM((1, own), jnp.int32),
            pltpu.VMEM((2, group, rows, 2 * keys), jnp.float32),
            pltpu.VMEM((group, rows, 128), jnp.float32),
            pltpu.VMEM((group, rows, 128), jnp.float32),
            pltpu.VMEM((group, rows, 128), jnp.float32),
            pltpu.VMEM((2, NX, 16, 128), jnp.float32),
            pltpu.VMEM((HALF, 1, keys), jnp.float32),
            pltpu.VMEM((HALF * NY, 1, keys), jnp.float32),
            pltpu.VMEM((keys // NY, width), jnp.bfloat16),
            dma(1), dma(1), dma(1), dma(4), dma(1), dma(1), dma(2), dma(1), dma(1), dma(1), dma(2), dma(1), dma(1), dma(1), dma(1), dma(1), pltpu.SemaphoreType.REGULAR((13,)),
        ],
        compiler_params=pltpu.CompilerParams(collective_id=0, has_side_effects=True, vmem_limit_bytes=58 << 20),
    )(queries[:, 0], key_cache[0], key_positions[None], span_end[None])
    return best


def solution(mesh):
    placed = (P(("qry", "ctx"), "head", None), P("head", "ctx", None), P("ctx"), P(("qry", "ctx")))
    return jax.shard_map(shards, mesh=mesh, in_specs=placed, out_specs=P("head", "ctx"), check_vma=False)
```

```python
import functools
import math

import jax
import jax.numpy as jnp
from jax import lax
from jax.experimental import pallas as pl
from jax.experimental.pallas import tpu as pltpu
from jax.sharding import PartitionSpec as P

NEG_FILL = -1e30
MESH = pl.DeviceIdType.MESH
NX, NY, NZ = 4, 4, 8
HALF = NZ // 2


def kernel(group, q_ref, k_ref, p_ref, e_ref, o_ref, qbuf, kbuf, pbuf, ebuf, sbuf, mst, lst, colb, st, cm, rbuf, kown,
           lk, lq, le, qr, qz, qs, kr, pr, ks, ps, yr, ys, ss, sr, cs, cr, ready):
    ctx, y = lax.axis_index("ctx"), lax.axis_index("qry")
    z, x = ctx // NX, lax.rem(ctx, NX)
    side = lax.rem(z, 2)
    twin = z + 1 - 2 * side
    half = z // HALF
    inside = side == half
    keys, width = k_ref.shape
    quarter = keys // NY
    rows = 2 * qbuf.shape[1] * qbuf.shape[2]
    scale = width**-0.5
    to_exp2 = math.log2(math.e) * scale
    mine = pl.ds(pl.multiple_of(y * quarter, quarter), quarter)

    def at(zz, xx):
        return {"ctx": zz * NX + xx}

    def turn(v, d):
        return lax.rem(v + d, 4)

    def remote(src, dst, send, recv, dev):
        return pltpu.make_async_remote_copy(src_ref=src, dst_ref=dst, send_sem=send, recv_sem=recv, device_id=dev, device_id_type=MESH)

    def drain(ref, sem):
        pltpu.make_async_copy(ref, ref, sem).wait()

    barrier = pltpu.get_barrier_semaphore()

    def greet(dev):
        pl.semaphore_signal(barrier, inc=1, device_id=dev, device_id_type=MESH)

    for j in range(HALF):
        source, target = HALF * side + j, 2 * j + half

        @pl.when(source > z)
        def _():
            greet(at(source, x))

        @pl.when(target > z)
        def _():
            greet(at(target, x))

    for v in range(1, 4):

        @pl.when(v > y)
        def _():
            greet({"qry": v})

        @pl.when(v > x)
        def _():
            greet(at(z, v))

    @pl.when(twin > z)
    def _():
        greet(at(twin, x))

    lower = jnp.clip(z - HALF * side, 0, HALF) + (z - half + 1) // 2
    waits = lower + x + y + side

    @pl.when(waits > 0)
    def _():
        pl.semaphore_wait(barrier, waits)


    def tell(index, dev):
        pl.semaphore_signal(ready.at[index], inc=1, device_id=dev, device_id_type=MESH)

    for j in range(HALF):
        source = HALF * side + j

        @pl.when(source < z)
        def _():
            tell(9 + z // 2, at(source, x))

    @pl.when(side == 1)
    def _():
        tell(8, at(twin, x))

    for v in range(3):

        @pl.when(v < x)
        def _():
            tell(x, at(z, v))

        @pl.when(v < y)
        def _():
            tell(4 + y, {"qry": v})

    pltpu.make_async_copy(q_ref, qbuf.at[side, x], lq.at[0]).start()
    pltpu.make_async_copy(e_ref, ebuf, le.at[0]).start()
    pltpu.make_async_copy(k_ref.at[mine], kown, lk.at[0]).start()
    slot = lax.rem(z, HALF)

    @pl.when(inside)
    def _():
        pltpu.make_async_copy(k_ref.at[mine], kbuf.at[y, slot], kr.at[slot // 2]).start()
        pltpu.make_async_copy(p_ref, pbuf.at[slot], pr.at[0]).start()

    def send_keys(target, block):
        remote(block, kbuf.at[y, slot], ks.at[0], kr.at[slot // 2], at(target, x)).start()
        remote(p_ref, pbuf.at[slot], ps.at[0], pr.at[0], at(target, x)).start()

    for i in range(HALF):
        target = 2 * i + half

        @pl.when(target < z)
        def _():
            send_keys(target, k_ref.at[mine])

    right, left = turn(x, 1), turn(x, 3)

    def send_twin():
        remote(q_ref, qbuf.at[side, x], qs.at[0], qz.at[0], at(twin, x)).start()

    pl.when(side == 1)(send_twin)
    for v in range(NX):
        if v:

            @pl.when(v > x)
            def _():
                pl.semaphore_wait(ready.at[v], 1)

        for index, near in ((0, right), (1, left)):

            @pl.when(v == near)
            def _():
                remote(q_ref, qbuf.at[side, x], qs.at[0], qr.at[index], at(z, v)).start()

    @pl.when(side == 0)
    def _():
        pl.semaphore_wait(ready.at[8], 1)
        send_twin()

    def send_later(near):
        for i in range(HALF):
            target = 2 * i + half

            @pl.when((target > z) & ((target <= z + 2) if near else (target > z + 2)))
            def _():
                pl.semaphore_wait(ready.at[9 + i], 1)
                send_keys(target, kown)

    drain(kown, lk.at[0])
    send_later(True)

    def forward(block, index, device):
        remote(block, block, qs.at[0], qr.at[index], at(z, device)).start()

    drain(q_ref, qr.at[1])
    forward(qbuf.at[side, right], 2, left)
    drain(q_ref, qz.at[0])
    for d in (1, 3, 2):
        forward(qbuf.at[1 - side, x], 3, turn(x, d))
    send_later(False)

    for v in range(1, NY):

        @pl.when(v > y)
        def _():
            pl.semaphore_wait(ready.at[4 + v], 1)

    def fan_out(g):
        drain(kbuf.at[0, pl.ds(0, 2)], kr.at[g])
        part = kbuf.at[y, pl.ds(2 * g, 2)]
        for d in (1, 3, 2):
            remote(part, part, ys.at[0], yr.at[g], {"qry": turn(y, d)}).start()

    st[side, x] = jnp.zeros(st.shape[2:], jnp.float32)
    flip = jnp.where((z == 4) | (z >= 6), 1, 0)
    fan_out(flip)
    fan_out(1 - flip)
    drain(q_ref, lq.at[0])
    drain(e_ref, le.at[0])
    drain(q_ref, qr.at[0])
    drain(q_ref, qr.at[2])
    drain(qbuf.at[0, pl.ds(0, NX - 1)], qr.at[3])
    drain(pbuf, pr.at[0])
    end = ebuf[0:1, 0:1]

    def bias_of(g):
        pos = jnp.concatenate([pbuf[2 * g], pbuf[2 * g + 1]], axis=1)
        return jnp.where(pos < end, 0.0, NEG_FILL)

    def scan_pair(step):
        g = 1 - flip if step else flip

        drain(kbuf.at[pl.ds(0, NY - 1), pl.ds(0, 2)], yr.at[g])
        parts = [kbuf[:, 2 * g + j].reshape(keys, width) for j in range(2)]
        bias = bias_of(g)
        for m in range(group):
            qm = qbuf[:, :, :, m * width : (m + 1) * width].reshape(rows, width)
            pieces = []
            for j, part in enumerate(parts):
                s = lax.dot_general(qm, part, (((1,), (1,)), ((), ())), preferred_element_type=jnp.float32)
                sbuf[g, m, :, j * keys : (j + 1) * keys] = s
                t = s + bias[:, j * keys : (j + 1) * keys]
                pieces += [t[:, c * 128 : (c + 1) * 128] for c in range(keys // 128)]
            if step:
                new = functools.reduce(jnp.maximum, pieces, mst[m])
                total = lst[m] * jnp.exp2((mst[m] - new) * to_exp2)
            else:
                new = functools.reduce(jnp.maximum, pieces)
                total = jnp.zeros_like(new)
            for piece in pieces:
                total = total + jnp.exp2((piece - new) * to_exp2)
            mst[m] = new
            lst[m] = total

    for step in range(2):
        scan_pair(step)

    blocks = [(m, b, m * (rows // 128) + b) for m in range(group) for b in range(rows // 128)]
    for m, b, r in blocks:
        tops, masses = mst[m, b * 128 : (b + 1) * 128].T, lst[m, b * 128 : (b + 1) * 128].T
        top = jnp.max(tops, axis=0, keepdims=True)
        mass = jnp.sum(masses * jnp.exp2((tops - top) * to_exp2), axis=0, keepdims=True)
        st[side, x, r : r + 1] = top + jnp.log(mass) * (1.0 / scale)
    own = st.at[side, x]
    for zz in (twin, z):
        for d in (2, 1, 3):
            remote(own, own, ss.at[0], sr.at[0], at(zz, turn(x, d))).start()
    remote(own, own, ss.at[0], sr.at[0], at(twin, x)).start()

    drain(sbuf.at[0, 0, pl.ds(0, 56), pl.ds(0, 256)], sr.at[0])
    levels = [st[e, i] for e in range(2) for i in range(NX)]
    top = functools.reduce(jnp.maximum, levels)
    mass = sum(jnp.exp2((a - top) * to_exp2) for a in levels)
    total = top + jnp.log(mass) * (1.0 / scale)
    for m, b, r in blocks:
        colb[m, b * 128 : (b + 1) * 128] = jnp.broadcast_to(total[r : r + 1], (128, 128)).T

    place = z // 2 * NY + y

    def best_pair(g, unused):
        def member(m, acc):
            for r in range(rows // 8):
                col = colb[m, r * 8 : (r + 1) * 8]
                acc = tuple(
                    jnp.maximum(a, sbuf[g, m, r * 8 : (r + 1) * 8, c * 128 : (c + 1) * 128] - col)
                    for c, a in enumerate(acc)
                )
            return acc

        start = tuple(jnp.full((8, 128), NEG_FILL, jnp.float32) for c in range(2 * keys // 128))
        acc = lax.fori_loop(0, group, member, start)
        best = jnp.concatenate([jnp.max(a, axis=0, keepdims=True) for a in acc], axis=1) * scale
        best = jnp.where(bias_of(g) < 0.0, NEG_FILL, best)
        cm[2 * g] = best[:, :keys]
        cm[2 * g + 1] = best[:, keys:]
        for j in range(2):
            far = 2 * g + j
            owner = HALF * side + far
            for d in range(NY):
                send = lambda: remote(cm.at[far], rbuf.at[place], cs.at[0], cr.at[0], {"ctx": owner * NX + x, "qry": turn(y, d)}).start()
                if d:
                    send()
                else:
                    pl.when(owner != z)(send)
        return unused

    for g in range(2):
        best_pair(g, 0)


    @pl.when(inside)
    def _():
        pltpu.make_async_copy(cm.at[slot], rbuf.at[place], cr.at[0]).start()

    drain(rbuf, cr.at[0])
    o_ref[...] = jnp.max(rbuf[...], axis=0)

    drain(sbuf.at[0, 0, pl.ds(0, 56), pl.ds(0, 256)], ss.at[0])
    drain(colb.at[pl.ds(0, 7), pl.ds(0, 112)], qs.at[0])
    drain(kbuf.at[pl.ds(0, 3)], ys.at[0])

    @pl.when(inside)
    def _():
        drain(rbuf.at[pl.ds(0, HALF * NY - 1)], cs.at[0])
        drain(kbuf.at[0, pl.ds(0, 3)], ks.at[0])
        drain(pbuf.at[pl.ds(0, 3)], ps.at[0])

    @pl.when(~inside)
    def _():
        drain(rbuf, cs.at[0])
        drain(kbuf.at[0], ks.at[0])
        drain(pbuf, ps.at[0])


def shards(queries, key_cache, key_positions, span_end):
    own, unused, lanes = queries.shape
    keys, width = key_cache.shape[1:]
    group = lanes // width
    rows = own * NX * 2
    dma = lambda n: pltpu.SemaphoreType.DMA((n,))
    best = pl.pallas_call(
        functools.partial(kernel, group),
        out_shape=jax.ShapeDtypeStruct((1, keys), jnp.float32),
        in_specs=[pl.BlockSpec(memory_space=pl.ANY)] * 4,
        out_specs=pl.BlockSpec(memory_space=pltpu.VMEM),
        scratch_shapes=[
            pltpu.VMEM((2, NX, own, lanes), jnp.bfloat16),
            pltpu.VMEM((NY, HALF, keys // NY, width), jnp.bfloat16),
            pltpu.VMEM((HALF, 1, keys), jnp.int32),
            pltpu.VMEM((1, own), jnp.int32),
            pltpu.VMEM((2, group, rows, 2 * keys), jnp.float32),
            pltpu.VMEM((group, rows, 128), jnp.float32),
            pltpu.VMEM((group, rows, 128), jnp.float32),
            pltpu.VMEM((group, rows, 128), jnp.float32),
            pltpu.VMEM((2, NX, 16, 128), jnp.float32),
            pltpu.VMEM((HALF, 1, keys), jnp.float32),
            pltpu.VMEM((HALF * NY, 1, keys), jnp.float32),
            pltpu.VMEM((keys // NY, width), jnp.bfloat16),
            dma(1), dma(1), dma(1), dma(4), dma(1), dma(1), dma(2), dma(1), dma(1), dma(1), dma(2), dma(1), dma(1), dma(1), dma(1), dma(1), pltpu.SemaphoreType.REGULAR((13,)),
        ],
        compiler_params=pltpu.CompilerParams(collective_id=0, has_side_effects=True, vmem_limit_bytes=58 << 20),
    )(queries[:, 0], key_cache[0], key_positions[None], span_end[None])
    return best


def solution(mesh):
    placed = (P(("qry", "ctx"), "head", None), P("head", "ctx", None), P("ctx"), P(("qry", "ctx")))
    return jax.shard_map(shards, mesh=mesh, in_specs=placed, out_specs=P("head", "ctx"), check_vma=False)
```
